256 devices in a mesh: ctx: 32 (over y, z), head: 8 (over x, core).
Axes of the slice: x: 4, y: 4, z: 8, core: 2. Of those that a mesh axis runs over, the one named last changes fastest.
Arguments:
- queries: bfloat16 [32768, 4096], P('ctx', 'head'), may hold values from -140 to 140
- keys: bfloat16 [32768, 1024], P('ctx', 'head'), may hold values from -8 to 8
- values: bfloat16 [32768, 1024], P('ctx', 'head'), may hold values from -6 to 6
- gates: int32 [32, 32, 3], P('ctx', 'head'), may hold values from 0 to 31, all different within a row; in each aligned block of 4 rows (0 to 3, 4 to 7, ..., all dimensions but the last counted through in order) at most 2 rows name the same one
- out_weight: bfloat16 [4096, 4096], P('head'), may hold values from -0.125 to 0.125
Outputs:
- attended: bfloat16 [32768, 4096], P('ctx', 'head')
The draws below stay inside these ranges and needn't reach their ends.
Inputs may be any that keep to these rules, and one draw needn't show every extreme that they name: `gates`: the 3 entries of one query block and head are distinct. Within one query block and one group of 4 consecutive heads no key block is named more than 2 times, and some key block is named exactly 2 times. An entry that is not smaller than its query block's index selects nothing.
All inputs are finite; a program needn't handle non-finite values.
Results may differ from the reference program's by a relative error of at most 0.019.
Values may be sent and summed in bfloat16 or wider, within the bound.
A program may use at most 192 MiB of HBM per device.

```python
import math
import jax
import jax.numpy as jnp
import numpy as np
from jax import lax

D = 4096
QUERY_HEADS = 32
KEY_VALUE_HEADS = 8
HEAD_SIZE = 128
BLOCK_TOKENS = 1024
TOPK = 3
BLOCK_COUNT = 32
SEQUENCE_TOKENS = 32768
HQ_DEV = 4
MOST = 2


def aligned_keys(key, mixing):
    base_values = jnp.clip(jax.random.normal(key, (SEQUENCE_TOKENS, KEY_VALUE_HEADS * HEAD_SIZE), jnp.float32), -6.0, 6.0)
    random_noise = jnp.clip(jax.random.normal(jax.random.fold_in(key, 101), (SEQUENCE_TOKENS, KEY_VALUE_HEADS * HEAD_SIZE), jnp.float32), -6.0, 6.0)
    marks = jax.random.bernoulli(jax.random.fold_in(key, 102), 1.0 / 64.0, (SEQUENCE_TOKENS,))
    marks = marks & (jnp.arange(SEQUENCE_TOKENS) % BLOCK_TOKENS != 0) & (mixing > 0.5)
    shifted = jnp.roll(base_values, 1, axis=0) + 0.15 * random_noise
    return (jnp.where(marks[:, None], shifted, base_values), marks)


def draw_keys(key, part):
    mixing = 0.0
    shared_component, marks = aligned_keys(key, mixing)
    return shared_component.astype(jnp.bfloat16)


def draw_queries(key, part):
    mixing = 0.0
    shared_component, marks = aligned_keys(key, mixing)
    key = jax.random.fold_in(key, 5)
    base_values = jnp.clip(jax.random.normal(key, (SEQUENCE_TOKENS, QUERY_HEADS * HEAD_SIZE), jnp.float32), -6.0, 6.0)
    strength = jax.random.uniform(jax.random.fold_in(key, 7), (SEQUENCE_TOKENS, 1), jnp.float32, 8.0, 20.0)
    spread_scale = jnp.broadcast_to(shared_component.reshape(SEQUENCE_TOKENS, KEY_VALUE_HEADS, 1, HEAD_SIZE), (SEQUENCE_TOKENS, KEY_VALUE_HEADS, QUERY_HEADS // KEY_VALUE_HEADS, HEAD_SIZE))
    aligned = strength * spread_scale.reshape(SEQUENCE_TOKENS, QUERY_HEADS * HEAD_SIZE)
    return jnp.where(marks[:, None], aligned, base_values).astype(jnp.bfloat16)


def strengthened(result, key, source, target, parts, factor):
    owner, partner = [(jnp.arange(result.shape[position]) // (result.shape[position] // parts)).reshape([-1 if axis == position else 1 for axis in range(result.ndim)]) for position in (source, target)]
    chosen = jax.random.permutation(key, parts)[partner]
    strong = (owner == chosen) | (owner == (partner + parts // 2) % parts)
    return jnp.where(strong, factor * result, result)


def steps_of(own_key, extent, shards, smallest, top_value):
    level, own = 1.0, jax.random.fold_in(own_key, 6)
    for axis_at, blocks in shards:
        draws = jnp.exp(jax.random.uniform(jax.random.fold_in(own, axis_at), (blocks,), jnp.float32, smallest / len(shards), top_value / len(shards)))
        level = level * jnp.repeat(draws, extent[axis_at] // blocks).reshape([-1 if axis == axis_at else 1 for axis in range(len(extent))])
    return level


def routed_block(own_key, own, number, rows, count, top, bound, slope):
    order = jax.random.permutation(own_key, count)
    crowded, ordinary = shares(count, rows * top, bound, slope, True), shares(count, rows * top, bound, slope, False)
    places = jnp.arange(count)

    def named(lengths, offset_by):
        used = int((lengths > 0).sum())
        fixed = max(1, used // 4)
        passed = fixed + (places - fixed + offset_by * (used - fixed)) % max(1, count - fixed)
        return jnp.zeros((count,), jnp.int32).at[order[jnp.where(places < fixed, places, passed)]].set(jnp.asarray(lengths, jnp.int32))

    lengths = jnp.where(number % 4 == 0, named(crowded, number // 4), named(ordinary, number - number // 4 - 1))
    mixed = jax.random.permutation(jax.random.fold_in(own, 3), count)
    donor, sink = mixed[0:count // 2 * 2:2], mixed[1:count // 2 * 2:2]
    slack = jnp.minimum(lengths[donor] - 1, bound - lengths[sink]) // 2
    slack = jnp.where((donor == order[0]) | (sink == order[0]) | (lengths[sink] == 0), 0, jnp.maximum(slack, 0))
    passed = jax.random.randint(jax.random.fold_in(own, 4), (count // 2,), 0, 1 << 20) % (slack + 1)
    lengths = lengths.at[donor].add(-passed).at[sink].add(passed)
    members = jnp.searchsorted(jnp.cumsum(lengths), jnp.arange(rows * top), side="right").astype(jnp.int32)
    grid = members.reshape(top, rows).T
    grid = grid[jax.random.permutation(jax.random.fold_in(own, 1), rows)]
    offset_by = jax.random.randint(jax.random.fold_in(own, 2), (rows, 1), 0, top)
    return jnp.take_along_axis(grid, (jnp.arange(top)[None, :] + offset_by) % top, axis=1)


def shares(count, total, limit, slope, full):
    weights = [(1 << 20) // math.isqrt(standing ** slope) + 1 for standing in range(1, count + 1)]
    largest = limit if full else min(limit, max(-(-total // count), total * weights[0] // sum(weights)))
    least = 1 if total - largest >= count - 1 else 0
    counts, rest = [largest] + [least] * (count - 1), total - largest - least * (count - 1)
    while rest > 0:
        movable = [i for i in range(1, count) if counts[i] < largest] or [i for i in range(1, count) if counts[i] < limit]
        whole, remaining = sum([weights[i] for i in movable]), rest
        for i in movable:
            extra = min(limit - counts[i], max(1, remaining * weights[i] // whole), rest)
            counts[i] = counts[i] + extra
            rest = rest - extra
    return np.array(counts)


def bell_draw(own_key, dims, spread, reach, shards=(), kind=jnp.bfloat16):
    result = jax.random.normal(own_key, dims, jnp.float32) * spread
    if len(shards) > 0:
        result = steps_of(own_key, dims, shards, -0.22, 0.18) * result
    return jnp.clip(result, min=-reach, max=reach).astype(kind)


def heavy_noise(stream_key, shape, scale, reach, pieces, heavy, kind=jnp.bfloat16):
    values = scale * jax.random.normal(stream_key, shape, jnp.float32)
    if pieces:
        values = values * steps_of(stream_key, shape, pieces, -0.22, 0.18)
    return jnp.clip(strengthened(values, jax.random.fold_in(stream_key, 3), *heavy), -reach, reach).astype(kind)


def setup_inputs(seed: int = 0) -> dict:
    seeds = jax.random.split(jax.random.key(seed), 6)
    queries = draw_queries(jax.random.fold_in(seeds[5], 71), 0)
    keys = draw_keys(jax.random.fold_in(seeds[5], 71), 0)
    values = bell_draw(seeds[2], (SEQUENCE_TOKENS, KEY_VALUE_HEADS * HEAD_SIZE), 1.0, 6.0, ((0, 32), (1, 8)))
    gates_keys = jax.random.split(jax.random.fold_in(seeds[3], 1), BLOCK_COUNT * QUERY_HEADS // HQ_DEV)
    gates_turns = jax.random.permutation(jax.random.fold_in(seeds[3], 3), BLOCK_COUNT * QUERY_HEADS // HQ_DEV)
    gates = jax.vmap(lambda own, number: routed_block(jax.random.fold_in(seeds[3], 2), own, number, HQ_DEV, BLOCK_COUNT, TOPK, MOST, 2))(gates_keys, gates_turns).reshape((BLOCK_COUNT, QUERY_HEADS, TOPK))
    out_weight = heavy_noise(seeds[4], (QUERY_HEADS * HEAD_SIZE, D), (QUERY_HEADS * HEAD_SIZE) ** -0.5, 0.125, ((0, 8),), (0, 1, 8, 2.0))
    return dict(queries=queries, keys=keys, values=values, gates=gates, out_weight=out_weight)


def block_attend(q_here, k_here, v_here, causal):
    scores = jnp.einsum("hqd,hkd->hqk", q_here.astype(jnp.float32), k_here.astype(jnp.float32))
    scores = scores * (HEAD_SIZE ** -0.5)
    if causal:
        places = jnp.arange(BLOCK_TOKENS)
        scores = jnp.where((places[:, None] >= places[None, :])[None], scores, -1e30)
    peak = jnp.max(scores, axis=2)
    expo = jnp.exp(scores - peak[:, :, None])
    total = jnp.sum(expo, axis=2)
    weights = expo.astype(jnp.bfloat16).astype(jnp.float32)
    mixed = jnp.einsum("hqk,hkd->hqd", weights, v_here.astype(jnp.float32))
    partial_out = (mixed / total[:, :, None]).astype(jnp.bfloat16)
    return partial_out, peak + jnp.log(total)


def reference(queries, keys, values, gates, out_weight):
    query_group_size = QUERY_HEADS // KEY_VALUE_HEADS
    q_rows = queries.reshape(BLOCK_COUNT, BLOCK_TOKENS, QUERY_HEADS, HEAD_SIZE)
    key_rows = keys.reshape(BLOCK_COUNT, BLOCK_TOKENS, KEY_VALUE_HEADS, HEAD_SIZE)
    value_rows = values.reshape(BLOCK_COUNT, BLOCK_TOKENS, KEY_VALUE_HEADS, HEAD_SIZE)
    kv_index = (jnp.arange(QUERY_HEADS) // query_group_size).astype(jnp.int32)

    def per_block(qblock):
        q_here = jnp.transpose(q_rows[qblock], (1, 0, 2))
        k_here = jnp.transpose(key_rows[qblock][:, kv_index, :], (1, 0, 2))
        v_here = jnp.transpose(value_rows[qblock][:, kv_index, :], (1, 0, 2))
        own_out, own_lse = block_attend(q_here, k_here, v_here, True)
        out_list = [own_out]
        lse_list = [own_lse]
        chosen = gates[qblock]
        for slot_pos in range(TOPK):
            picked = chosen[:, slot_pos]
            k_sel = key_rows[picked, :, kv_index, :]
            v_sel = value_rows[picked, :, kv_index, :]
            sel_out, sel_lse = block_attend(q_here, k_sel, v_sel, False)
            sel_lse = jnp.where((picked < qblock)[:, None], sel_lse, -1e30)
            out_list.append(sel_out)
            lse_list.append(sel_lse)
        lse_all = jnp.stack(lse_list, 0)
        out_all = jnp.stack(out_list, 0).astype(jnp.float32)
        peak = jnp.max(lse_all, axis=0)
        weight = jnp.exp(lse_all - peak[None])
        merged = jnp.sum(weight[..., None] * out_all, axis=0) / jnp.sum(weight, axis=0)[..., None]
        return jnp.transpose(merged.astype(jnp.bfloat16), (1, 0, 2)).reshape(BLOCK_TOKENS, QUERY_HEADS * HEAD_SIZE)

    attention = lax.map(per_block, jnp.arange(BLOCK_COUNT, dtype=jnp.int32)).reshape(SEQUENCE_TOKENS, QUERY_HEADS * HEAD_SIZE)
    group_count = QUERY_HEADS // HQ_DEV
    width = HQ_DEV * HEAD_SIZE
    summed = jnp.zeros((SEQUENCE_TOKENS, D), jnp.float32)
    for group in range(group_count):
        columns = attention[:, group * width:(group + 1) * width]
        weight_rows = out_weight[group * width:(group + 1) * width]
        term = jnp.dot(columns, weight_rows, preferred_element_type=jnp.float32).astype(jnp.bfloat16)
        term = lax.optimization_barrier(term)
        summed = summed + term.astype(jnp.float32)
    return summed.astype(jnp.bfloat16)
```

```python
import functools

import jax
import jax.numpy as jnp
from jax import lax
from jax.experimental import pallas as pl
from jax.experimental.pallas import tpu as pltpu
from jax.sharding import PartitionSpec as P

MESH = pl.DeviceIdType.MESH
F32 = jnp.float32
BF16 = jnp.bfloat16
TOK = 1024
HS = 128
HQ = 4
TOPK = 3
NY = 4
NZ = 8
NX = 4
SCALE2 = HS**-0.5 * 1.4426950408889634
LOW = -1e30
VMEM_LIMIT = 56 * 1024 * 1024
QCH = 4


def dev(ctx, head):
    return (ctx, head)


def gather_kernel(q_ref, k_ref, v_ref, g_ref, qa, ka, va, ga, kv_s, kv_r, q_s, q_r, g_s, g_r, loc):
    ctx = lax.axis_index("ctx")
    head = lax.axis_index("head")
    y = ctx // NZ
    z = ctx % NZ
    up = y * NZ + (z + 1) % NZ
    down = y * NZ + (z + NZ - 1) % NZ
    column = [((y + d) % NY) * NZ + z for d in (1, 2, 3)]

    barrier = pltpu.get_barrier_semaphore()
    for other in [up, down] + column:
        pl.semaphore_signal(barrier, inc=1, device_id=dev(other, head), device_id_type=MESH)
    pl.semaphore_wait(barrier, 5)

    def remote(src, dst, s, r, to):
        return pltpu.make_async_remote_copy(
            src_ref=src, dst_ref=dst, send_sem=s, recv_sem=r, device_id=dev(to, head), device_id_type=MESH
        )

    def ring_copy(direction, step, part):
        block = (z + NZ - step) % NZ if direction == 0 else (z + step) % NZ
        own, out = (k_ref, ka) if part == 0 else (v_ref, va)
        src = own if step == 0 else out.at[block]
        return remote(
            src, out.at[block], kv_s.at[direction, step, part], kv_r.at[direction, step, part], up if direction == 0 else down
        )

    def parts(direction, step):
        return (0, 1) if step < 3 else (direction,)

    own_copies = [
        pltpu.make_async_copy(k_ref, ka.at[z], loc.at[0]),
        pltpu.make_async_copy(v_ref, va.at[z], loc.at[1]),
        pltpu.make_async_copy(q_ref, qa.at[0], loc.at[2]),
        pltpu.make_async_copy(g_ref, ga.at[0], loc.at[3]),
    ]
    rows = TOK // QCH

    def q_copy(kind, c):
        at = pl.ds(c * rows, rows)
        if kind == 0:
            return remote(q_ref.at[at], qa.at[1, at], q_s.at[0, c], q_r.at[0, c], column[2])
        if kind == 1:
            return remote(qa.at[1, at], qa.at[2, at], q_s.at[1, c], q_r.at[1, c], column[2])
        return remote(q_ref.at[at], qa.at[3, at], q_s.at[2, c], q_r.at[2, c], column[0])

    for part in (0, 1):
        for direction in (0, 1):
            ring_copy(direction, 0, part).start()

    @pl.when(y >= 1)
    def _():
        for c in range(QCH):
            q_copy(0, c).start()

    @pl.when(y == NY - 1)
    def _():
        for c in range(QCH):
            q_copy(2, c).start()

    g_copies = [remote(g_ref, ga.at[NY - d], g_s.at[d - 1], g_r.at[d - 1], column[d - 1]) for d in (1, 2, 3)]
    for c in g_copies:
        c.start()
    for c in own_copies:
        c.start()

    for step in range(4):
        for part in (0, 1):
            for direction in (0, 1):
                if part in parts(direction, step):
                    ring_copy(direction, step, part).wait_recv()
                    if step < 3 and part in parts(direction, step + 1):
                        ring_copy(direction, step + 1, part).start()
        if step < 3:

            @pl.when((y >= 1) & (y + 1 < NY))
            def _(step=step):
                for c in (step,) if step < 2 else (2, 3):
                    q_copy(0, c).wait_recv()
                    q_copy(1, c).start()

    @pl.when(y == 0)
    def _():
        for c in range(QCH):
            q_copy(0, c).wait_recv()
            q_copy(2, c).wait_recv()

    @pl.when(y + 2 < NY)
    def _():
        for c in range(QCH):
            q_copy(1, c).wait_recv()

    @pl.when(y >= 1)
    def _():
        for c in range(QCH):
            q_copy(0, c).wait_send()

    @pl.when((y >= 1) & (y + 1 < NY))
    def _():
        for c in range(QCH):
            q_copy(1, c).wait_send()

    @pl.when(y == NY - 1)
    def _():
        for c in range(QCH):
            q_copy(2, c).wait_send()

    for step in range(4):
        for direction in (0, 1):
            for part in parts(direction, step):
                ring_copy(direction, step, part).wait_send()
    for c in g_copies:
        c.wait()
    for c in own_copies:
        c.wait()


def gather(q, k, v, g):
    hbm = pl.BlockSpec(memory_space=pl.ANY)
    return pl.pallas_call(
        gather_kernel,
        out_shape=(
            jax.ShapeDtypeStruct((NY, TOK, HQ * HS), BF16),
            jax.ShapeDtypeStruct((NZ, TOK, HS), BF16),
            jax.ShapeDtypeStruct((NZ, TOK, HS), BF16),
            jax.ShapeDtypeStruct((NY, 8, 128), jnp.int32),
        ),
        in_specs=[hbm] * 4,
        out_specs=(hbm,) * 4,
        scratch_shapes=[
            pltpu.SemaphoreType.DMA((2, 4, 2)),
            pltpu.SemaphoreType.DMA((2, 4, 2)),
            pltpu.SemaphoreType.DMA((3, QCH)),
            pltpu.SemaphoreType.DMA((3, QCH)),
            pltpu.SemaphoreType.DMA((3,)),
            pltpu.SemaphoreType.DMA((3,)),
            pltpu.SemaphoreType.DMA((4,)),
        ],
        compiler_params=pltpu.CompilerParams(
            collective_id=0, has_side_effects=True, vmem_limit_bytes=VMEM_LIMIT
        ),
        name="gather",
    )(q, k, v, g)


RT = 256


def attend_kernel(gates, place, q_ref, k_ref, v_ref, out_ref, lse_ref, peak, acc, todo):
    slot = pl.program_id(0)
    head = pl.program_id(1)
    y = place[0]
    z = place[1]
    mine = (y + slot) * NZ + z

    def tile(i, k_tile, v_ext, first, diagonal):
        at = pl.ds(i * RT, RT)
        s = lax.dot_general(
            q_ref[0, at, :], k_tile, (((1,), (1,)), ((), ())), preferred_element_type=F32
        )
        if diagonal:
            keys = k_tile.shape[0]
            r = lax.broadcasted_iota(jnp.int32, (RT, keys), 0) + (keys - RT)
            c = lax.broadcasted_iota(jnp.int32, (RT, keys), 1)
            s = jnp.where(r >= c, s, LOW)
        top = jnp.max(s, axis=1, keepdims=True) * SCALE2
        if first:
            new = jnp.broadcast_to(top, (RT, HS))
        else:
            old = peak[at, :]
            new = jnp.maximum(old, top)
        p = jnp.exp2(s * SCALE2 - new[:, :1]).astype(BF16)
        part = jnp.dot(p, v_ext, preferred_element_type=F32)
        if first:
            acc[at, :] = part
        else:
            fade = jnp.exp2(old - new)
            acc[at, :] = acc[at, :] * jnp.concatenate([fade, fade], axis=1) + part
        peak[at, :] = new

    def extended(block, n):
        v = v_ref[block, 0:n, :]
        return jnp.concatenate([v, jnp.ones_like(v)], axis=1)

    count = jnp.int32(0)
    for j in range(TOPK):
        g = gates[slot * (HQ * TOPK) + head * TOPK + j]
        good = (g >= y * NZ) & (g < (y + 1) * NZ) & (g < mine) & (y + slot < NY)

        @pl.when(good)
        def _(g=g, count=count):
            todo[count] = g - y * NZ

        count = count + good.astype(jnp.int32)

    @pl.when(slot == 0)
    def _():
        for i in range(TOK // RT):
            n = (i + 1) * RT
            tile(i, k_ref[z, 0:n, :], extended(z, n), True, True)

    @pl.when((slot > 0) & (count > 0))
    def _():
        block = todo[0]
        for i in range(TOK // RT):
            tile(i, k_ref[block], extended(block, TOK), True, False)

    def more(e, carry):
        block = todo[e]
        for i in range(TOK // RT):
            tile(i, k_ref[block], extended(block, TOK), False, False)
        return carry

    lax.fori_loop(jnp.where(slot == 0, 0, 1), count, more, 0)

    some = (slot == 0) | (count > 0)

    @pl.when(some)
    def _():
        for i in range(TOK // RT):
            at = pl.ds(i * RT, RT)
            total = acc[at, HS:]
            out_ref[0, at, :] = (acc[at, :HS] / total).astype(BF16)
            lse = peak[at, :] + jnp.log2(total)
            lse_ref[0, pl.ds(head, 1), at] = lse.T[0:1, :]

    @pl.when(jnp.logical_not(some))
    def _():
        out_ref[...] = jnp.zeros_like(out_ref)
        lse_ref[0, pl.ds(head, 1), :] = jnp.full((1, TOK), LOW, F32)


def attend(gates, place, qa, ka, va):
    return pl.pallas_call(
        attend_kernel,
        out_shape=(
            jax.ShapeDtypeStruct((NY, TOK, HQ * HS), BF16),
            jax.ShapeDtypeStruct((NY, 8, TOK), F32),
        ),
        grid_spec=pltpu.PrefetchScalarGridSpec(
            num_scalar_prefetch=2,
            grid=(NY, HQ),
            in_specs=[
                pl.BlockSpec((1, TOK, HS), lambda s, h, *_: (s, 0, h)),
                pl.BlockSpec((NZ, TOK, HS), lambda s, h, *_: (0, 0, 0)),
                pl.BlockSpec((NZ, TOK, HS), lambda s, h, *_: (0, 0, 0)),
            ],
            out_specs=(
                pl.BlockSpec((1, TOK, HS), lambda s, h, *_: (s, 0, h)),
                pl.BlockSpec((1, 8, TOK), lambda s, h, *_: (s, 0, 0)),
            ),
            scratch_shapes=[
                pltpu.VMEM((TOK, HS), F32),
                pltpu.VMEM((TOK, 2 * HS), F32),
                pltpu.SMEM((TOPK + 1,), jnp.int32),
            ],
        ),
        compiler_params=pltpu.CompilerParams(vmem_limit_bytes=VMEM_LIMIT),
        name="attend",
    )(gates, place, qa, ka, va)


NC = 8
CR = TOK // NC
HF = CR // 2


def project_kernel(a_ref, w_ref, out_ref, sib_out, sib_in, own, a_out, a_in, b_out, b_in, ss, sr, as_, ar, bs, br):
    ctx = lax.axis_index("ctx")
    head = lax.axis_index("head")
    x = head // 2
    core = head % 2
    sibling = x * 2 + (1 - core)
    right = ((x + 1) % NX) * 2 + core
    left = ((x + NX - 1) % NX) * 2 + core
    beside = [right, left]
    width = HQ * HS

    barrier = pltpu.get_barrier_semaphore()
    for other in [sibling, right, left]:
        pl.semaphore_signal(barrier, inc=1, device_id=dev(ctx, other), device_id_type=MESH)
    pl.semaphore_wait(barrier, 3)

    def remote(src, dst, s, r, to):
        return pltpu.make_async_remote_copy(
            src_ref=src, dst_ref=dst, send_sem=s, recv_sem=r, device_id=dev(ctx, to), device_id_type=MESH
        )

    def sib_copy(r):
        return remote(sib_out.at[r], sib_in.at[r], ss.at[r], sr.at[r], sibling)

    def a_copy(r, side):
        return remote(a_out.at[r, side], a_in.at[r, side], as_.at[r, side], ar.at[r, side], beside[side])

    def b_copy(r, side):
        return remote(b_out.at[r, side], b_in.at[r, side], bs.at[r, side], br.at[r, side], beside[side])

    def columns(k, c):
        return pl.ds(pl.multiple_of((((x + k) % NX) * 2 + c) * width, width), width)

    def stage0(r):
        rows = a_ref[pl.ds(pl.multiple_of(r * CR, CR), CR), :]
        for k in range(NX):
            t = jnp.dot(rows, w_ref[:, columns(k, 1 - core)], preferred_element_type=F32)
            sib_out[r, k] = t.astype(BF16)
        sib_copy(r).start()
        for k in range(NX):
            own[r, k] = jnp.dot(rows, w_ref[:, columns(k, core)], preferred_element_type=F32).astype(BF16)

    def pair(r, k, at):
        return own[r, k, at, :].astype(F32) + sib_in[r, k, at, :].astype(F32)

    def stage1(r):
        sib_copy(r).wait_recv()
        for side in (0, 1):
            a_out[r, side] = pair(r, 2, pl.ds(side * HF, HF)).astype(BF16)
            a_copy(r, side).start()

    def stage2(r):
        for side in (0, 1):
            k = 1 if side == 0 else 3
            a_copy(r, side).wait_recv()
            with_a = pl.ds(side * HF, HF)
            without = pl.ds((1 - side) * HF, HF)
            b_out[r, side, with_a, :] = (pair(r, k, with_a) + a_in[r, side].astype(F32)).astype(BF16)
            b_out[r, side, without, :] = pair(r, k, without).astype(BF16)
            b_copy(r, side).start()

    def stage3(r):
        b_copy(r, 0).wait_recv()
        b_copy(r, 1).wait_recv()
        total = pair(r, 0, pl.ds(0, CR)) + b_in[r, 0].astype(F32) + b_in[r, 1].astype(F32)
        out_ref[pl.ds(pl.multiple_of(r * CR, CR), CR), :] = total.astype(BF16)

    def step(t, carry):
        @pl.when(t < NC)
        def _():
            stage0(t)

        @pl.when((t >= 1) & (t < NC + 1))
        def _():
            stage1(t - 1)

        @pl.when((t >= 2) & (t < NC + 2))
        def _():
            stage2(t - 2)

        @pl.when(t >= 3)
        def _():
            stage3(t - 3)

        return carry

    lax.fori_loop(0, NC + 3, step, 0)

    def finish(r, carry):
        sib_copy(r).wait_send()
        for side in (0, 1):
            a_copy(r, side).wait_send()
            b_copy(r, side).wait_send()
        return carry

    lax.fori_loop(0, NC, finish, 0)


def project(attention, weight):
    width = HQ * HS
    vmem = pl.BlockSpec(memory_space=pltpu.VMEM)
    return pl.pallas_call(
        project_kernel,
        out_shape=jax.ShapeDtypeStruct((TOK, width), BF16),
        in_specs=[vmem] * 2,
        out_specs=vmem,
        scratch_shapes=[
            pltpu.VMEM((NC, NX, CR, width), BF16),
            pltpu.VMEM((NC, NX, CR, width), BF16),
            pltpu.VMEM((NC, NX, CR, width), BF16),
            pltpu.VMEM((NC, 2, HF, width), BF16),
            pltpu.VMEM((NC, 2, HF, width), BF16),
            pltpu.VMEM((NC, 2, CR, width), BF16),
            pltpu.VMEM((NC, 2, CR, width), BF16),
            pltpu.SemaphoreType.DMA((NC,)),
            pltpu.SemaphoreType.DMA((NC,)),
            pltpu.SemaphoreType.DMA((NC, 2)),
            pltpu.SemaphoreType.DMA((NC, 2)),
            pltpu.SemaphoreType.DMA((NC, 2)),
            pltpu.SemaphoreType.DMA((NC, 2)),
        ],
        compiler_params=pltpu.CompilerParams(
            collective_id=1, has_side_effects=True, vmem_limit_bytes=VMEM_LIMIT
        ),
        name="project",
    )(attention, weight)


def merge(partial, lse):
    y = lax.axis_index("ctx") // NZ
    outs = [partial[0]]
    lses = [lse[0, :HQ]]
    for d in (1, 2, 3):
        pairs = [((yy * NZ + zz), ((yy + d) % NY) * NZ + zz) for yy in range(NY) for zz in range(NZ)]
        got = lax.ppermute(partial[d], "ctx", pairs)
        got_lse = lax.ppermute(lse[d], "ctx", pairs)
        outs.append(got)
        lses.append(jnp.where(y >= d, got_lse[:HQ], LOW))
    lses = jnp.stack(lses, 0)
    top = jnp.max(lses, axis=0)
    w = jnp.exp2(lses - top[None])
    w = w / jnp.sum(w, axis=0)[None]
    total = 0.0
    for d in range(NY):
        wide = jnp.repeat(w[d].T, HS, axis=1)
        total = total + wide * outs[d].astype(F32)
    return total.astype(BF16)


def shards(queries, keys, values, gates, out_weight):
    ctx = lax.axis_index("ctx")
    padded = jnp.zeros((8, 128), jnp.int32).at[0, : HQ * TOPK].set(gates.reshape(-1))
    qa, ka, va, ga = gather(queries, keys, values, padded)
    flat = ga[:, 0, : HQ * TOPK].reshape(-1)
    place = jnp.stack([ctx // NZ, ctx % NZ]).astype(jnp.int32)
    partial, lse = attend(flat, place, qa, ka, va)
    return project(merge(partial, lse), out_weight)


def solution(mesh):
    return jax.shard_map(
        shards,
        mesh=mesh,
        in_specs=(
            P("ctx", "head"),
            P("ctx", "head"),
            P("ctx", "head"),
            P("ctx", "head", None),
            P("head", None),
        ),
        out_specs=P("ctx", "head"),
        check_vma=False,
    )
```

```python
import functools

import jax
import jax.numpy as jnp
from jax import lax
from jax.experimental import pallas as pl
from jax.experimental.pallas import tpu as pltpu
from jax.sharding import PartitionSpec as P

MESH = pl.DeviceIdType.MESH
F32 = jnp.float32
BF16 = jnp.bfloat16
TOK = 1024
HS = 128
HQ = 4
TOPK = 3
NY = 4
NZ = 8
NX = 4
SCALE2 = HS**-0.5 * 1.4426950408889634
LOW = -1e30
VMEM_LIMIT = 56 * 1024 * 1024
QCH = 4


def dev(ctx, head):
    return (ctx, head)


def gather_kernel(q_ref, k_ref, v_ref, g_ref, qa, ka, va, ga, kv_s, kv_r, q_s, q_r, g_s, g_r, loc):
    ctx = lax.axis_index("ctx")
    head = lax.axis_index("head")
    y = ctx // NZ
    z = ctx % NZ
    up = y * NZ + (z + 1) % NZ
    down = y * NZ + (z + NZ - 1) % NZ
    column = [((y + d) % NY) * NZ + z for d in (1, 2, 3)]

    barrier = pltpu.get_barrier_semaphore()
    for other in [up, down] + column:
        pl.semaphore_signal(barrier, inc=1, device_id=dev(other, head), device_id_type=MESH)
    pl.semaphore_wait(barrier, 5)

    def remote(src, dst, s, r, to):
        return pltpu.make_async_remote_copy(
            src_ref=src, dst_ref=dst, send_sem=s, recv_sem=r, device_id=dev(to, head), device_id_type=MESH
        )

    def ring_copy(direction, step, part):
        block = (z + NZ - step) % NZ if direction == 0 else (z + step) % NZ
        own, out = (k_ref, ka) if part == 0 else (v_ref, va)
        src = own if step == 0 else out.at[block]
        return remote(
            src, out.at[block], kv_s.at[direction, step, part], kv_r.at[direction, step, part], up if direction == 0 else down
        )

    def parts(direction, step):
        return (0, 1) if step < 3 else (direction,)

    own_copies = [
        pltpu.make_async_copy(k_ref, ka.at[z], loc.at[0]),
        pltpu.make_async_copy(v_ref, va.at[z], loc.at[1]),
        pltpu.make_async_copy(q_ref, qa.at[0], loc.at[2]),
        pltpu.make_async_copy(g_ref, ga.at[0], loc.at[3]),
    ]
    rows = TOK // QCH

    def q_copy(kind, c):
        at = pl.ds(c * rows, rows)
        if kind == 0:
            return remote(q_ref.at[at], qa.at[1, at], q_s.at[0, c], q_r.at[0, c], column[2])
        if kind == 1:
            return remote(qa.at[1, at], qa.at[2, at], q_s.at[1, c], q_r.at[1, c], column[2])
        return remote(q_ref.at[at], qa.at[3, at], q_s.at[2, c], q_r.at[2, c], column[0])

    for part in (0, 1):
        for direction in (0, 1):
            ring_copy(direction, 0, part).start()

    @pl.when(y >= 1)
    def _():
        for c in range(QCH):
            q_copy(0, c).start()

    @pl.when(y == NY - 1)
    def _():
        for c in range(QCH):
            q_copy(2, c).start()

    g_copies = [remote(g_ref, ga.at[NY - d], g_s.at[d - 1], g_r.at[d - 1], column[d - 1]) for d in (1, 2, 3)]
    for c in g_copies:
        c.start()
    for c in own_copies:
        c.start()

    for step in range(4):
        for part in (0, 1):
            for direction in (0, 1):
                if part in parts(direction, step):
                    ring_copy(direction, step, part).wait_recv()
                    if step < 3 and part in parts(direction, step + 1):
                        ring_copy(direction, step + 1, part).start()
        if step < 3:

            @pl.when((y >= 1) & (y + 1 < NY))
            def _(step=step):
                for c in (step,) if step < 2 else (2, 3):
                    q_copy(0, c).wait_recv()
                    q_copy(1, c).start()

    @pl.when(y == 0)
    def _():
        for c in range(QCH):
            q_copy(0, c).wait_recv()
            q_copy(2, c).wait_recv()

    @pl.when(y + 2 < NY)
    def _():
        for c in range(QCH):
            q_copy(1, c).wait_recv()

    @pl.when(y >= 1)
    def _():
        for c in range(QCH):
            q_copy(0, c).wait_send()

    @pl.when((y >= 1) & (y + 1 < NY))
    def _():
        for c in range(QCH):
            q_copy(1, c).wait_send()

    @pl.when(y == NY - 1)
    def _():
        for c in range(QCH):
            q_copy(2, c).wait_send()

    for step in range(4):
        for direction in (0, 1):
            for part in parts(direction, step):
                ring_copy(direction, step, part).wait_send()
    for c in g_copies:
        c.wait()
    for c in own_copies:
        c.wait()


def gather(q, k, v, g):
    hbm = pl.BlockSpec(memory_space=pl.ANY)
    return pl.pallas_call(
        gather_kernel,
        out_shape=(
            jax.ShapeDtypeStruct((NY, TOK, HQ * HS), BF16),
            jax.ShapeDtypeStruct((NZ, TOK, HS), BF16),
            jax.ShapeDtypeStruct((NZ, TOK, HS), BF16),
            jax.ShapeDtypeStruct((NY, 8, 128), jnp.int32),
        ),
        in_specs=[hbm] * 4,
        out_specs=(hbm,) * 4,
        scratch_shapes=[
            pltpu.SemaphoreType.DMA((2, 4, 2)),
            pltpu.SemaphoreType.DMA((2, 4, 2)),
            pltpu.SemaphoreType.DMA((3, QCH)),
            pltpu.SemaphoreType.DMA((3, QCH)),
            pltpu.SemaphoreType.DMA((3,)),
            pltpu.SemaphoreType.DMA((3,)),
            pltpu.SemaphoreType.DMA((4,)),
        ],
        compiler_params=pltpu.CompilerParams(
            collective_id=0, has_side_effects=True, vmem_limit_bytes=VMEM_LIMIT
        ),
        name="gather",
    )(q, k, v, g)


RT = 256


def attend_kernel(gates, place, q_ref, k_ref, v_ref, out_ref, lse_ref, peak, acc, todo):
    slot = pl.program_id(0)
    head = pl.program_id(1)
    y = place[0]
    z = place[1]
    mine = (y + slot) * NZ + z

    def tile(i, k_tile, v_ext, first, diagonal):
        at = pl.ds(i * RT, RT)
        s = lax.dot_general(
            q_ref[0, at, :], k_tile, (((1,), (1,)), ((), ())), preferred_element_type=F32
        )
        if diagonal:
            keys = k_tile.shape[0]
            r = lax.broadcasted_iota(jnp.int32, (RT, keys), 0) + (keys - RT)
            c = lax.broadcasted_iota(jnp.int32, (RT, keys), 1)
            s = jnp.where(r >= c, s, LOW)
        top = jnp.max(s, axis=1, keepdims=True) * SCALE2
        if first:
            new = jnp.broadcast_to(top, (RT, HS))
        else:
            old = peak[at, :]
            new = jnp.maximum(old, top)
        p = jnp.exp2(s * SCALE2 - new[:, :1]).astype(BF16)
        part = jnp.dot(p, v_ext, preferred_element_type=F32)
        if first:
            acc[at, :] = part
        else:
            fade = jnp.exp2(old - new)
            acc[at, :] = acc[at, :] * jnp.concatenate([fade, fade], axis=1) + part
        peak[at, :] = new

    def extended(block, n):
        v = v_ref[block, 0:n, :]
        return jnp.concatenate([v, jnp.ones_like(v)], axis=1)

    count = jnp.int32(0)
    for j in range(TOPK):
        g = gates[slot * (HQ * TOPK) + head * TOPK + j]
        good = (g >= y * NZ) & (g < (y + 1) * NZ) & (g < mine) & (y + slot < NY)

        @pl.when(good)
        def _(g=g, count=count):
            todo[count] = g - y * NZ

        count = count + good.astype(jnp.int32)

    @pl.when(slot == 0)
    def _():
        for i in range(TOK // RT):
            n = (i + 1) * RT
            tile(i, k_ref[z, 0:n, :], extended(z, n), True, True)

    @pl.when((slot > 0) & (count > 0))
    def _():
        block = todo[0]
        for i in range(TOK // RT):
            tile(i, k_ref[block], extended(block, TOK), True, False)

    def more(e, carry):
        block = todo[e]
        for i in range(TOK // RT):
            tile(i, k_ref[block], extended(block, TOK), False, False)
        return carry

    lax.fori_loop(jnp.where(slot == 0, 0, 1), count, more, 0)

    some = (slot == 0) | (count > 0)

    @pl.when(some)
    def _():
        for i in range(TOK // RT):
            at = pl.ds(i * RT, RT)
            total = acc[at, HS:]
            out_ref[0, at, :] = (acc[at, :HS] / total).astype(BF16)
            lse = peak[at, :] + jnp.log2(total)
            lse_ref[0, pl.ds(head, 1), at] = lse.T[0:1, :]

    @pl.when(jnp.logical_not(some))
    def _():
        out_ref[...] = jnp.zeros_like(out_ref)
        lse_ref[0, pl.ds(head, 1), :] = jnp.full((1, TOK), LOW, F32)


def attend(gates, place, qa, ka, va):
    return pl.pallas_call(
        attend_kernel,
        out_shape=(
            jax.ShapeDtypeStruct((NY, TOK, HQ * HS), BF16),
            jax.ShapeDtypeStruct((NY, 8, TOK), F32),
        ),
        grid_spec=pltpu.PrefetchScalarGridSpec(
            num_scalar_prefetch=2,
            grid=(NY, HQ),
            in_specs=[
                pl.BlockSpec((1, TOK, HS), lambda s, h, *_: (s, 0, h)),
                pl.BlockSpec((NZ, TOK, HS), lambda s, h, *_: (0, 0, 0)),
                pl.BlockSpec((NZ, TOK, HS), lambda s, h, *_: (0, 0, 0)),
            ],
            out_specs=(
                pl.BlockSpec((1, TOK, HS), lambda s, h, *_: (s, 0, h)),
                pl.BlockSpec((1, 8, TOK), lambda s, h, *_: (s, 0, 0)),
            ),
            scratch_shapes=[
                pltpu.VMEM((TOK, HS), F32),
                pltpu.VMEM((TOK, 2 * HS), F32),
                pltpu.SMEM((TOPK + 1,), jnp.int32),
            ],
        ),
        compiler_params=pltpu.CompilerParams(vmem_limit_bytes=VMEM_LIMIT),
        name="attend",
    )(gates, place, qa, ka, va)


NC = 8
CR = TOK // NC
HF = CR // 2
LOOK = 2
WIDTH = HQ * HS


def spread(w):
    t = w.T
    return jnp.concatenate([jnp.broadcast_to(t[:, h : h + 1], (t.shape[0], HS)) for h in range(HQ)], axis=1)


def join(sources):
    top = functools.reduce(jnp.maximum, [l for l, _ in sources])
    ws = [jnp.exp2(l - top) for l, _ in sources]
    total = functools.reduce(jnp.add, ws)
    inv = 1.0 / total
    mixed = functools.reduce(jnp.add, [spread(w * inv) * p.astype(F32) for w, (_, p) in zip(ws, sources)])
    return mixed.astype(BF16), top + jnp.log2(total)


def project_kernel(
    p_ref, l_ref, w_hbm, out_ref,
    w_ref, p0, p1, r1, r2, r3, m1, l1, l2, l3, lm, att, sib_out, sib_in, own, a_out, a_in, b_out, b_in,
    loc, ps, pr, ls, lr, ss, sr, as_, ar, bs, br,
):
    ctx = lax.axis_index("ctx")
    head = lax.axis_index("head")
    y = ctx // NZ
    z = ctx % NZ
    x = head // 2
    core = head % 2
    sibling = x * 2 + (1 - core)
    right = ((x + 1) % NX) * 2 + core
    left = ((x + NX - 1) % NX) * 2 + core
    beside = [right, left]
    above = ((y + 1) % NY) * NZ + z
    below = ((y + NY - 1) % NY) * NZ + z

    local = [
        pltpu.make_async_copy(p_ref.at[0], p0, loc.at[0]),
        pltpu.make_async_copy(p_ref.at[1], p1, loc.at[1]),
        pltpu.make_async_copy(w_hbm, w_ref, loc.at[2]),
    ]
    for c in local:
        c.start()

    barrier = pltpu.get_barrier_semaphore()
    for other in [(ctx, sibling), (ctx, right), (ctx, left), (above, head), (below, head)]:
        pl.semaphore_signal(barrier, inc=1, device_id=other, device_id_type=MESH)
    pl.semaphore_wait(barrier, 5)

    def remote(src, dst, s, r, to):
        return pltpu.make_async_remote_copy(
            src_ref=src, dst_ref=dst, send_sem=s, recv_sem=r, device_id=to, device_id_type=MESH
        )

    def rows_of(r):
        return pl.ds(pl.multiple_of(r * CR, CR), CR)

    def ret_copies(kind, r, merged=False):
        at = rows_of(r)
        dst, ldst = ((r1, l1), (r2, l2), (r3, l3))[kind]
        if merged:
            src, lsrc = m1.at[at], lm.at[r]
        else:
            src, lsrc = p_ref.at[kind + 1, at], l_ref.at[kind + 1, :, at]
        to = (below if kind == 2 else above, head)
        return [
            remote(src, dst.at[at], ps.at[kind, r], pr.at[kind, r], to),
            remote(lsrc, ldst.at[r], ls.at[kind, r], lr.at[kind, r], to),
        ]

    def send_plain(r):
        @pl.when(y + 2 < NY)
        def _():
            for c in ret_copies(1, r):
                c.start()

        @pl.when(y == 0)
        def _():
            for c in ret_copies(0, r) + ret_copies(2, r):
                c.start()

    def relay(r):
        @pl.when((y >= 1) & (y + 1 < NY))
        def _():
            for c in ret_copies(1, r):
                c.wait_recv()
            at = rows_of(r)
            mixed, lse = join([(l_own(1, r), p1[at, :]), (l2[r], r2[at, :])])
            m1[at, :] = mixed
            lm[r] = lse
            for c in ret_copies(0, r, True):
                c.start()

    def l_own(slot, r):
        return l_ref[slot, :, rows_of(r)]

    def home(r):
        at = rows_of(r)

        @pl.when(y == 0)
        def _():
            att[...] = p0[at, :]

        @pl.when((y >= 1) & (y + 1 < NY))
        def _():
            for c in ret_copies(0, r):
                c.wait_recv()
            att[...] = join([(l_own(0, r), p0[at, :]), (l1[r], r1[at, :])])[0]

        @pl.when(y == NY - 1)
        def _():
            for c in ret_copies(0, r) + ret_copies(2, r):
                c.wait_recv()
            att[...] = join([(l_own(0, r), p0[at, :]), (l1[r], r1[at, :]), (l3[r], r3[at, :])])[0]

    def sib_copy(r):
        return remote(sib_out.at[r], sib_in.at[r], ss.at[r], sr.at[r], (ctx, sibling))

    def a_copy(r, side):
        return remote(a_out.at[r, side], a_in.at[r, side], as_.at[r, side], ar.at[r, side], (ctx, beside[side]))

    def b_copy(r, side):
        return remote(b_out.at[r, side], b_in.at[r, side], bs.at[r, side], br.at[r, side], (ctx, beside[side]))

    def columns(k, c):
        return pl.ds(pl.multiple_of((((x + k) % NX) * 2 + c) * WIDTH, WIDTH), WIDTH)

    def stage0(r):
        home(r)
        rows = att[...]
        for k in range(NX):
            t = jnp.dot(rows, w_ref[:, columns(k, 1 - core)], preferred_element_type=F32)
            sib_out[r, k] = t.astype(BF16)
        sib_copy(r).start()
        for k in range(NX):
            own[r, k] = jnp.dot(rows, w_ref[:, columns(k, core)], preferred_element_type=F32).astype(BF16)

    def pair(r, k, at):
        return own[r, k, at, :].astype(F32) + sib_in[r, k, at, :].astype(F32)

    def stage1(r):
        sib_copy(r).wait_recv()
        for side in (0, 1):
            a_out[r, side] = pair(r, 2, pl.ds(side * HF, HF)).astype(BF16)
            a_copy(r, side).start()

    def stage2(r):
        for side in (0, 1):
            k = 1 if side == 0 else 3
            a_copy(r, side).wait_recv()
            with_a = pl.ds(side * HF, HF)
            without = pl.ds((1 - side) * HF, HF)
            b_out[r, side, with_a, :] = (pair(r, k, with_a) + a_in[r, side].astype(F32)).astype(BF16)
            b_out[r, side, without, :] = pair(r, k, without).astype(BF16)
            b_copy(r, side).start()

    def stage3(r):
        b_copy(r, 0).wait_recv()
        b_copy(r, 1).wait_recv()
        total = pair(r, 0, pl.ds(0, CR)) + b_in[r, 0].astype(F32) + b_in[r, 1].astype(F32)
        out_ref[rows_of(r), :] = total.astype(BF16)

    def when(cond, f, r):
        @pl.when(cond)
        def _():
            f(r)

    for r in range(LOOK):
        send_plain(r)
    for c in local:
        c.wait()
    relay(0)

    def step(t, carry):
        when(t + LOOK < NC, send_plain, t + LOOK)
        when(t + 1 < NC, relay, t + 1)
        when(t < NC, stage0, t)
        when((t >= 1) & (t < NC + 1), stage1, t - 1)
        when((t >= 2) & (t < NC + 2), stage2, t - 2)
        when(t >= 3, stage3, t - 3)
        return carry

    lax.fori_loop(0, NC + 3, step, 0)

    def finish(r, carry):
        @pl.when(y + 1 < NY)
        def _():
            for c in ret_copies(0, r):
                c.wait_send()

        @pl.when(y + 2 < NY)
        def _():
            for c in ret_copies(1, r):
                c.wait_send()

        @pl.when(y == 0)
        def _():
            for c in ret_copies(2, r):
                c.wait_send()

        sib_copy(r).wait_send()
        for side in (0, 1):
            a_copy(r, side).wait_send()
            b_copy(r, side).wait_send()
        return carry

    lax.fori_loop(0, NC, finish, 0)


def project(partial, lse, weight):
    vmem = pl.BlockSpec(memory_space=pltpu.VMEM)
    hbm = pl.BlockSpec(memory_space=pl.ANY)
    sem = pltpu.SemaphoreType.DMA
    return pl.pallas_call(
        project_kernel,
        out_shape=jax.ShapeDtypeStruct((TOK, WIDTH), BF16),
        in_specs=[hbm, vmem, hbm],
        out_specs=vmem,
        scratch_shapes=[
            pltpu.VMEM(weight.shape, BF16),
            *[pltpu.VMEM((TOK, WIDTH), BF16)] * 6,
            *[pltpu.VMEM((NC, 8, CR), F32)] * 4,
            pltpu.VMEM((CR, WIDTH), BF16),
            pltpu.VMEM((NC, NX, CR, WIDTH), BF16),
            pltpu.VMEM((NC, NX, CR, WIDTH), BF16),
            pltpu.VMEM((NC, NX, CR, WIDTH), BF16),
            pltpu.VMEM((NC, 2, HF, WIDTH), BF16),
            pltpu.VMEM((NC, 2, HF, WIDTH), BF16),
            pltpu.VMEM((NC, 2, CR, WIDTH), BF16),
            pltpu.VMEM((NC, 2, CR, WIDTH), BF16),
            sem((3,)),
            *[sem((3, NC))] * 4,
            *[sem((NC,))] * 2,
            *[sem((NC, 2))] * 4,
        ],
        compiler_params=pltpu.CompilerParams(
            collective_id=1, has_side_effects=True, vmem_limit_bytes=VMEM_LIMIT
        ),
        name="project",
    )(partial, lse, weight)


def shards(queries, keys, values, gates, out_weight):
    ctx = lax.axis_index("ctx")
    padded = jnp.zeros((8, 128), jnp.int32).at[0, : HQ * TOPK].set(gates.reshape(-1))
    qa, ka, va, ga = gather(queries, keys, values, padded)
    flat = ga[:, 0, : HQ * TOPK].reshape(-1)
    place = jnp.stack([ctx // NZ, ctx % NZ]).astype(jnp.int32)
    partial, lse = attend(flat, place, qa, ka, va)
    return project(partial, lse, out_weight)


def solution(mesh):
    return jax.shard_map(
        shards,
        mesh=mesh,
        in_specs=(
            P("ctx", "head"),
            P("ctx", "head"),
            P("ctx", "head"),
            P("ctx", "head", None),
            P("head", None),
        ),
        out_specs=P("ctx", "head"),
        check_vma=False,
    )
```

```python
import functools

import jax
import jax.numpy as jnp
from jax import lax
from jax.experimental import pallas as pl
from jax.experimental.pallas import tpu as pltpu
from jax.sharding import PartitionSpec as P

MESH = pl.DeviceIdType.MESH
F32 = jnp.float32
BF16 = jnp.bfloat16
TOK = 1024
HS = 128
HQ = 4
TOPK = 3
NY = 4
NZ = 8
NX = 4
SCALE2 = HS**-0.5 * 1.4426950408889634
LOW = -1e30
VMEM_LIMIT = 56 * 1024 * 1024
QCH = 4


RT = 256
NT = TOK // RT
SAFE = 2.0**100
WIDTH = HQ * HS


def at(i):
    return pl.ds(i * RT, RT)


def wide(m, n):
    return jnp.concatenate([m] * (n // HS), axis=1)


def raw_scores(q, k):
    return lax.dot_general(q, k, (((1,), (1,)), ((), ())), preferred_element_type=F32)


def row_max(s):
    return jnp.broadcast_to(jnp.max(s, axis=1, keepdims=True) * SCALE2, (s.shape[0], HS))


def weights(s, m):
    return jnp.exp2(s * SCALE2 - wide(m, s.shape[1])).astype(BF16)


def as_row(m):
    eye = lax.broadcasted_iota(jnp.int32, (HS, HS), 0) == lax.broadcasted_iota(jnp.int32, (HS, HS), 1)
    pieces = [
        jnp.sum(jnp.where(eye, m[r : r + HS], 0.0), axis=0, keepdims=True) for r in range(0, m.shape[0], HS)
    ]
    return jnp.concatenate(pieces, axis=1)


def dev(ctx, head):
    return (ctx, head)


def gather_kernel(
    q_ref, k_ref, v_ref, g_ref, qa, ka, va, ga, oc, lc, vx, ov, lv, kv_s, kv_r, q_s, q_r, g_s, g_r, loc, res
):
    ctx = lax.axis_index("ctx")
    head = lax.axis_index("head")
    y = ctx // NZ
    z = ctx % NZ
    up = y * NZ + (z + 1) % NZ
    down = y * NZ + (z + NZ - 1) % NZ
    column = [((y + d) % NY) * NZ + z for d in (1, 2, 3)]

    barrier = pltpu.get_barrier_semaphore()
    for other in [up, down] + column:
        pl.semaphore_signal(barrier, inc=1, device_id=dev(other, head), device_id_type=MESH)
    pl.semaphore_wait(barrier, 5)

    def remote(src, dst, s, r, to):
        return pltpu.make_async_remote_copy(
            src_ref=src, dst_ref=dst, send_sem=s, recv_sem=r, device_id=dev(to, head), device_id_type=MESH
        )

    def ring_copy(direction, step, part):
        block = (z + NZ - step) % NZ if direction == 0 else (z + step) % NZ
        own, out = (k_ref, ka) if part == 0 else (v_ref, va)
        src = own if step == 0 else out.at[block]
        return remote(
            src, out.at[block], kv_s.at[direction, step, part], kv_r.at[direction, step, part], up if direction == 0 else down
        )

    def parts(direction, step):
        return (0, 1) if step < 3 else (direction,)

    own_copies = [
        pltpu.make_async_copy(k_ref, ka.at[z], loc.at[0]),
        pltpu.make_async_copy(v_ref, va.at[z], loc.at[1]),
        pltpu.make_async_copy(q_ref, qa.at[0], loc.at[2]),
        pltpu.make_async_copy(g_ref, ga.at[0], loc.at[3]),
    ]
    rows = TOK // QCH

    def q_copy(kind, c):
        at = pl.ds(c * rows, rows)
        if kind == 0:
            return remote(q_ref.at[at], qa.at[1, at], q_s.at[0, c], q_r.at[0, c], column[2])
        if kind == 1:
            return remote(qa.at[1, at], qa.at[2, at], q_s.at[1, c], q_r.at[1, c], column[2])
        return remote(q_ref.at[at], qa.at[3, at], q_s.at[2, c], q_r.at[2, c], column[0])

    for part in (0, 1):
        for direction in (0, 1):
            ring_copy(direction, 0, part).start()

    @pl.when(y >= 1)
    def _():
        for c in range(QCH):
            q_copy(0, c).start()

    @pl.when(y == NY - 1)
    def _():
        for c in range(QCH):
            q_copy(2, c).start()

    g_copies = [remote(g_ref, ga.at[NY - d], g_s.at[d - 1], g_r.at[d - 1], column[d - 1]) for d in (1, 2, 3)]
    for c in g_copies:
        c.start()
    for c in own_copies:
        c.start()

    vx[:, :HS] = v_ref[...]
    vx[:, HS:] = jnp.ones((TOK, HS), BF16)

    def result_copies(h):
        return [
            pltpu.make_async_copy(ov.at[:, pl.ds(h * HS, HS)], oc.at[:, pl.ds(h * HS, HS)], res.at[0, h]),
            pltpu.make_async_copy(lv.at[h], lc.at[h], res.at[1, h]),
        ]

    def causal(h):
        lanes = pl.ds(h * HS, HS)
        for i in range(NT):
            n = (i + 1) * RT
            s = raw_scores(q_ref[at(i), lanes], k_ref[0:n, :])
            r = lax.broadcasted_iota(jnp.int32, (RT, n), 0) + (n - RT)
            c = lax.broadcasted_iota(jnp.int32, (RT, n), 1)
            s = jnp.where(r >= c, s, LOW)
            m = row_max(s)
            mixed = jnp.dot(weights(s, m), vx[0:n, :], preferred_element_type=F32)
            total = mixed[:, HS:]
            ov[at(i), lanes] = (mixed[:, :HS] * (1.0 / total)).astype(BF16)
            lv[h, at(i), :] = m + jnp.log2(total)
        for c in result_copies(h):
            c.start()

    for step in range(4):
        for part in (0, 1):
            if 2 * step + part < HQ:
                causal(2 * step + part)
            for direction in (0, 1):
                if part in parts(direction, step):
                    ring_copy(direction, step, part).wait_recv()
                    if step < 3 and part in parts(direction, step + 1):
                        ring_copy(direction, step + 1, part).start()
        if step < 3:

            @pl.when((y >= 1) & (y + 1 < NY))
            def _(step=step):
                for c in (step,) if step < 2 else (2, 3):
                    q_copy(0, c).wait_recv()
                    q_copy(1, c).start()

    @pl.when(y == 0)
    def _():
        for c in range(QCH):
            q_copy(0, c).wait_recv()
            q_copy(2, c).wait_recv()

    @pl.when(y + 2 < NY)
    def _():
        for c in range(QCH):
            q_copy(1, c).wait_recv()

    @pl.when(y >= 1)
    def _():
        for c in range(QCH):
            q_copy(0, c).wait_send()

    @pl.when((y >= 1) & (y + 1 < NY))
    def _():
        for c in range(QCH):
            q_copy(1, c).wait_send()

    @pl.when(y == NY - 1)
    def _():
        for c in range(QCH):
            q_copy(2, c).wait_send()

    for step in range(4):
        for direction in (0, 1):
            for part in parts(direction, step):
                ring_copy(direction, step, part).wait_send()
    for c in g_copies:
        c.wait()
    for c in own_copies:
        c.wait()
    for h in range(HQ):
        for c in result_copies(h):
            c.wait()


def gather(q, k, v, g):
    hbm = pl.BlockSpec(memory_space=pl.ANY)
    return pl.pallas_call(
        gather_kernel,
        out_shape=(
            jax.ShapeDtypeStruct((NY, TOK, HQ * HS), BF16),
            jax.ShapeDtypeStruct((NZ, TOK, HS), BF16),
            jax.ShapeDtypeStruct((NZ, TOK, HS), BF16),
            jax.ShapeDtypeStruct((NY, 8, 128), jnp.int32),
            jax.ShapeDtypeStruct((TOK, WIDTH), BF16),
            jax.ShapeDtypeStruct((HQ, TOK, HS), F32),
        ),
        in_specs=[pl.BlockSpec(memory_space=pltpu.VMEM)] * 4,
        out_specs=(hbm,) * 6,
        scratch_shapes=[
            pltpu.VMEM((TOK, 2 * HS), BF16),
            pltpu.VMEM((TOK, WIDTH), BF16),
            pltpu.VMEM((HQ, TOK, HS), F32),
            pltpu.SemaphoreType.DMA((2, 4, 2)),
            pltpu.SemaphoreType.DMA((2, 4, 2)),
            pltpu.SemaphoreType.DMA((3, QCH)),
            pltpu.SemaphoreType.DMA((3, QCH)),
            pltpu.SemaphoreType.DMA((3,)),
            pltpu.SemaphoreType.DMA((3,)),
            pltpu.SemaphoreType.DMA((4,)),
            pltpu.SemaphoreType.DMA((2, HQ)),
        ],
        compiler_params=pltpu.CompilerParams(
            collective_id=0, has_side_effects=True, vmem_limit_bytes=VMEM_LIMIT
        ),
        name="gather",
    )(q, k, v, g)


def attend_kernel(
    gates, place, q_hbm, k_hbm, v_hbm, oc_hbm, lc_hbm, out_hbm, lse_ref,
    q_ref, k_ref, vx, oc_ref, lc_ref, out_ref, peak, acc, todo, sems, out_sems,
):
    y = place[0]
    z = place[1]

    shared = [
        pltpu.make_async_copy(k_hbm, k_ref, sems.at[0]),
        pltpu.make_async_copy(v_hbm, vx.at[:, :, pl.ds(0, HS)], sems.at[1]),
        pltpu.make_async_copy(oc_hbm, oc_ref, sems.at[2]),
        pltpu.make_async_copy(lc_hbm, lc_ref, sems.at[3]),
    ]

    def query_copy(slot):
        return pltpu.make_async_copy(q_hbm.at[slot], q_ref.at[slot], sems.at[4 + slot])

    def out_copy(slot):
        return pltpu.make_async_copy(out_ref.at[slot], out_hbm.at[slot], out_sems.at[slot])

    query_copy(0).start()
    for c in shared:
        c.start()
    for slot in range(1, NY):
        query_copy(slot).start()

    lse_ref[...] = jnp.full(lse_ref.shape, LOW, F32)

    def fill(block, carry):
        vx[block, :, HS:] = jnp.ones((TOK, HS), BF16)
        return carry

    lax.fori_loop(0, NZ, fill, 0)
    for c in shared:
        c.wait()

    def one(index, carry):
        slot = index // HQ
        head = index % HQ
        mine = (y + slot) * NZ + z
        lanes = pl.ds(pl.multiple_of(head * HS, HS), HS)

        @pl.when(head == 0)
        def _():
            query_copy(slot).wait()

        def scores(i, block):
            return raw_scores(q_ref[slot, at(i), lanes], k_ref[block])

        def mix(s, m, block):
            return jnp.dot(weights(s, m), vx[block], preferred_element_type=F32)

        count = jnp.int32(0)
        for j in range(TOPK):
            g = gates[slot * (HQ * TOPK) + head * TOPK + j]
            good = (g >= y * NZ) & (g < (y + 1) * NZ) & (g < mine) & (y + slot < NY)

            @pl.when(good)
            def _(g=g, count=count):
                todo[count] = g - y * NZ

            count = count + good.astype(jnp.int32)

        def start():
            @pl.when(slot == 0)
            def _():
                peak[...] = lc_ref[head]
                acc[:, :HS] = oc_ref[:, lanes].astype(F32)
                acc[:, HS:] = jnp.ones((TOK, HS), F32)

        def more(e, carry):
            block = todo[e]
            for i in range(NT):
                acc[at(i), :] += mix(scores(i, block), peak[at(i), :], block)
            return carry

        def general(e, carry):
            block = todo[e]
            for i in range(NT):
                s = scores(i, block)
                old = peak[at(i), :]
                new = jnp.maximum(old, row_max(s))
                peak[at(i), :] = new
                acc[at(i), :] = acc[at(i), :] * wide(jnp.exp2(old - new), 2 * HS) + mix(s, new, block)
            return carry

        @pl.when(count > 0)
        def _():
            start()

            @pl.when(slot > 0)
            def _():
                block = todo[0]
                for i in range(NT):
                    s = scores(i, block)
                    m = row_max(s[:, :RT])
                    peak[at(i), :] = m
                    acc[at(i), :] = mix(s, m, block)

            lax.fori_loop(jnp.where(slot == 0, 0, 1), count, more, 0)
            fine = jnp.min((acc[:, HS:] < SAFE).astype(F32)) > 0.5

            @pl.when(jnp.logical_not(fine))
            def _():
                peak[...] = jnp.full(peak.shape, LOW, F32)
                acc[...] = jnp.zeros_like(acc)
                start()
                lax.fori_loop(0, count, general, 0)

            for i in range(NT):
                total = acc[at(i), HS:]
                out_ref[slot, at(i), lanes] = (acc[at(i), :HS] * (1.0 / total)).astype(BF16)
                lse_ref[slot, pl.ds(head, 1), at(i)] = as_row(peak[at(i), :] + jnp.log2(total))

        @pl.when((count == 0) & (slot == 0))
        def _():
            out_ref[slot, :, lanes] = oc_ref[:, lanes]
            for i in range(NT):
                lse_ref[slot, pl.ds(head, 1), at(i)] = as_row(lc_ref[head, at(i), :])

        @pl.when((count == 0) & (slot > 0))
        def _():
            out_ref[slot, :, lanes] = jnp.zeros((TOK, HS), BF16)

        @pl.when(head == HQ - 1)
        def _():
            out_copy(slot).start()

        return carry

    lax.fori_loop(0, NY * HQ, one, 0)
    for slot in range(NY):
        out_copy(slot).wait()


def attend(gates, place, qa, ka, va, oc, lc):
    hbm = pl.BlockSpec(memory_space=pl.ANY)
    smem = pl.BlockSpec(memory_space=pltpu.SMEM)
    return pl.pallas_call(
        attend_kernel,
        out_shape=(
            jax.ShapeDtypeStruct((NY, TOK, WIDTH), BF16),
            jax.ShapeDtypeStruct((NY, 8, TOK), F32),
        ),
        in_specs=[smem, smem] + [hbm] * 5,
        out_specs=(hbm, pl.BlockSpec(memory_space=pltpu.VMEM)),
        scratch_shapes=[
            pltpu.VMEM((NY, TOK, WIDTH), BF16),
            pltpu.VMEM((NZ, TOK, HS), BF16),
            pltpu.VMEM((NZ, TOK, 2 * HS), BF16),
            pltpu.VMEM((TOK, WIDTH), BF16),
            pltpu.VMEM((HQ, TOK, HS), F32),
            pltpu.VMEM((NY, TOK, WIDTH), BF16),
            pltpu.VMEM((TOK, HS), F32),
            pltpu.VMEM((TOK, 2 * HS), F32),
            pltpu.SMEM((TOPK + 1,), jnp.int32),
            pltpu.SemaphoreType.DMA((4 + NY,)),
            pltpu.SemaphoreType.DMA((NY,)),
        ],
        compiler_params=pltpu.CompilerParams(vmem_limit_bytes=VMEM_LIMIT),
        name="attend",
    )(gates, place, qa, ka, va, oc, lc)


NC = 8
CR = TOK // NC
HF = CR // 2
LOOK = 3
HALF = WIDTH // 2
LEFT_HALF = slice(0, HALF)
RIGHT_HALF = slice(HALF, WIDTH)


def join(sources, heads):
    top = functools.reduce(jnp.maximum, [l for l, _ in sources])
    ws = [jnp.exp2(l - top) for l, _ in sources]
    total = functools.reduce(jnp.add, ws)
    inv = 1.0 / total
    mixed = 0.0
    for w, (_, p) in zip(ws, sources):
        t = (w * inv).T
        wide_w = jnp.concatenate([jnp.broadcast_to(t[:, h : h + 1], (t.shape[0], HS)) for h in heads], axis=1)
        mixed = mixed + wide_w * p.astype(F32)
    return mixed.astype(BF16), top + jnp.log2(total)


def project_kernel(
    p_ref, l_ref, w_hbm, out_ref,
    w_ref, p0, p1, p3, r1, r2, r3, r4, r5, m1, m3, l1, l2, l3, l4, l5, lm1, lm3, att,
    sib_out, sib_in, own, a_out, a_in, b_out, b_in,
    loc, ps, pr, ls, lr, ss, sr, as_, ar, bs, br,
):
    ctx = lax.axis_index("ctx")
    head = lax.axis_index("head")
    y = ctx // NZ
    z = ctx % NZ
    x = head // 2
    core = head % 2
    sibling = x * 2 + (1 - core)
    right = ((x + 1) % NX) * 2 + core
    left = ((x + NX - 1) % NX) * 2 + core
    beside = [right, left]
    above = ((y + 1) % NY) * NZ + z
    below = ((y + NY - 1) % NY) * NZ + z

    local = [
        pltpu.make_async_copy(p_ref.at[0], p0, loc.at[0]),
        pltpu.make_async_copy(p_ref.at[1], p1, loc.at[1]),
        pltpu.make_async_copy(p_ref.at[3], p3, loc.at[2]),
        pltpu.make_async_copy(w_hbm, w_ref, loc.at[3]),
    ]
    for c in local:
        c.start()

    barrier = pltpu.get_barrier_semaphore()
    for other in [(ctx, sibling), (ctx, right), (ctx, left), (above, head), (below, head)]:
        pl.semaphore_signal(barrier, inc=1, device_id=other, device_id_type=MESH)
    pl.semaphore_wait(barrier, 5)

    def remote(src, dst, s, r, to):
        return pltpu.make_async_remote_copy(
            src_ref=src, dst_ref=dst, send_sem=s, recv_sem=r, device_id=to, device_id_type=MESH
        )

    def rows_of(r):
        return pl.ds(pl.multiple_of(r * CR, CR), CR)

    def stream(kind, r, merged=False):
        at = rows_of(r)
        first, second = pl.ds(0, HALF), pl.ds(HALF, HALF)
        own_lse = l_ref.at[min(kind, 2) + 1 if kind != 2 else 2, :, at]
        if kind == 0:
            src, lsrc = (m1.at[at], lm1.at[r]) if merged else (p_ref.at[1, at], own_lse)
            dst, ldst = r1.at[at], l1.at[r]
        elif kind == 1:
            src, lsrc, dst, ldst = p_ref.at[2, at, first], own_lse, r2.at[at], l2.at[r]
        elif kind == 2:
            src, lsrc, dst, ldst = p_ref.at[2, at, second], own_lse, r4.at[at], l4.at[r]
        elif kind == 3:
            src, lsrc, dst, ldst = m3.at[at], lm3.at[r], r3.at[at], l3.at[r]
        else:
            src, lsrc, dst, ldst = r4.at[at], l4.at[r], r5.at[at], l5.at[r]
        to = (above if kind < 2 else below, head)
        return [
            remote(src, dst, ps.at[kind, r], pr.at[kind, r], to),
            remote(lsrc, ldst, ls.at[kind, r], lr.at[kind, r], to),
        ]

    def begin(copies):
        for c in copies:
            c.start()

    def arrived(copies):
        for c in copies:
            c.wait_recv()

    def l_own(slot, r):
        return l_ref[slot, :, rows_of(r)]

    def pick(low, high):
        rows = lax.broadcasted_iota(jnp.int32, low.shape, 0)
        return jnp.where(rows < HQ // 2, low, high)

    def send_plain(r):
        @pl.when(y < 2)
        def _():
            begin(stream(2, r))
            begin(stream(1, r))

        @pl.when(y == 0)
        def _():
            begin(stream(0, r))

    def relay(r):
        at = rows_of(r)

        @pl.when((y == 1) | (y == 2))
        def _():
            arrived(stream(1, r))
            mixed, lse = join([(l_own(1, r), p1[at, LEFT_HALF]), (l2[r], r2[at, :])], (0, 1))
            m1[at, LEFT_HALF] = mixed
            m1[at, RIGHT_HALF] = p1[at, RIGHT_HALF]
            lm1[r] = pick(lse, l_own(1, r))
            begin(stream(0, r, True))

        @pl.when(y == 0)
        def _():
            arrived(stream(2, r))
            mixed, lse = join([(l_own(3, r), p3[at, RIGHT_HALF]), (l4[r], r4[at, :])], (2, 3))
            m3[at, RIGHT_HALF] = mixed
            m3[at, LEFT_HALF] = p3[at, LEFT_HALF]
            lm3[r] = pick(l_own(3, r), lse)
            begin(stream(3, r))

        @pl.when(y == 3)
        def _():
            arrived(stream(2, r))
            begin(stream(4, r))

    def home(r):
        at = rows_of(r)

        @pl.when(y == 0)
        def _():
            att[...] = p0[at, :]

        @pl.when(y == 1)
        def _():
            arrived(stream(0, r))
            att[...] = join([(l_own(0, r), p0[at, :]), (l1[r], r1[at, :])], range(HQ))[0]

        @pl.when(y == 2)
        def _():
            arrived(stream(0, r) + stream(4, r))
            own_lse = l_own(0, r)
            att[:, LEFT_HALF] = join([(own_lse, p0[at, LEFT_HALF]), (l1[r], r1[at, LEFT_HALF])], (0, 1))[0]
            att[:, RIGHT_HALF] = join(
                [(own_lse, p0[at, RIGHT_HALF]), (l1[r], r1[at, RIGHT_HALF]), (l5[r], r5[at, :])], (2, 3)
            )[0]

        @pl.when(y == 3)
        def _():
            arrived(stream(0, r) + stream(3, r))
            att[...] = join([(l_own(0, r), p0[at, :]), (l1[r], r1[at, :]), (l3[r], r3[at, :])], range(HQ))[0]

    def sib_copy(r):
        return remote(sib_out.at[r], sib_in.at[r], ss.at[r], sr.at[r], (ctx, sibling))

    def a_copy(r, side):
        return remote(a_out.at[r, side], a_in.at[r, side], as_.at[r, side], ar.at[r, side], (ctx, beside[side]))

    def b_copy(r, side):
        return remote(b_out.at[r, side], b_in.at[r, side], bs.at[r, side], br.at[r, side], (ctx, beside[side]))

    def columns(k, c):
        return pl.ds(pl.multiple_of((((x + k) % NX) * 2 + c) * WIDTH, WIDTH), WIDTH)

    def stage0(r):
        home(r)
        rows = att[...]
        for k in range(NX):
            t = jnp.dot(rows, w_ref[:, columns(k, 1 - core)], preferred_element_type=F32)
            sib_out[r, k] = t.astype(BF16)
        sib_copy(r).start()
        for k in range(NX):
            own[r, k] = jnp.dot(rows, w_ref[:, columns(k, core)], preferred_element_type=F32).astype(BF16)

    def pair(r, k, at):
        return own[r, k, at, :].astype(F32) + sib_in[r, k, at, :].astype(F32)

    def stage1(r):
        sib_copy(r).wait_recv()
        for side in (0, 1):
            a_out[r, side] = pair(r, 2, pl.ds(side * HF, HF)).astype(BF16)
            a_copy(r, side).start()

    def stage2(r):
        for side in (0, 1):
            k = 1 if side == 0 else 3
            a_copy(r, side).wait_recv()
            with_a = pl.ds(side * HF, HF)
            without = pl.ds((1 - side) * HF, HF)
            b_out[r, side, with_a, :] = (pair(r, k, with_a) + a_in[r, side].astype(F32)).astype(BF16)
            b_out[r, side, without, :] = pair(r, k, without).astype(BF16)
            b_copy(r, side).start()

    def stage3(r):
        b_copy(r, 0).wait_recv()
        b_copy(r, 1).wait_recv()
        total = pair(r, 0, pl.ds(0, CR)) + b_in[r, 0].astype(F32) + b_in[r, 1].astype(F32)
        out_ref[rows_of(r), :] = total.astype(BF16)

    def when(cond, f, r):
        @pl.when(cond)
        def _():
            f(r)

    for r in range(LOOK):
        send_plain(r)
    for c in local:
        c.wait()
    relay(0)

    def step(t, carry):
        when(t + LOOK < NC, send_plain, t + LOOK)
        when(t + 1 < NC, relay, t + 1)
        when(t < NC, stage0, t)
        when((t >= 1) & (t < NC + 1), stage1, t - 1)
        when((t >= 2) & (t < NC + 2), stage2, t - 2)
        when(t >= 3, stage3, t - 3)
        return carry

    lax.fori_loop(0, NC + 3, step, 0)

    def sent(copies):
        for c in copies:
            c.wait_send()

    def finish(r, carry):
        @pl.when(y < 3)
        def _():
            sent(stream(0, r))

        @pl.when(y < 2)
        def _():
            sent(stream(1, r) + stream(2, r))

        @pl.when(y == 0)
        def _():
            sent(stream(3, r))

        @pl.when(y == 3)
        def _():
            sent(stream(4, r))

        sib_copy(r).wait_send()
        for side in (0, 1):
            a_copy(r, side).wait_send()
            b_copy(r, side).wait_send()
        return carry

    lax.fori_loop(0, NC, finish, 0)


def project(partial, lse, weight):
    vmem = pl.BlockSpec(memory_space=pltpu.VMEM)
    hbm = pl.BlockSpec(memory_space=pl.ANY)
    sem = pltpu.SemaphoreType.DMA
    full = pltpu.VMEM((TOK, WIDTH), BF16)
    half = pltpu.VMEM((TOK, HALF), BF16)
    return pl.pallas_call(
        project_kernel,
        out_shape=jax.ShapeDtypeStruct((TOK, WIDTH), BF16),
        in_specs=[hbm, vmem, hbm],
        out_specs=vmem,
        scratch_shapes=[
            pltpu.VMEM(weight.shape, BF16),
            full, full, full,
            full, half, full, half, half,
            full, full,
            *[pltpu.VMEM((NC, 8, CR), F32)] * 7,
            pltpu.VMEM((CR, WIDTH), BF16),
            pltpu.VMEM((NC, NX, CR, WIDTH), BF16),
            pltpu.VMEM((NC, NX, CR, WIDTH), BF16),
            pltpu.VMEM((NC, NX, CR, WIDTH), BF16),
            pltpu.VMEM((NC, 2, HF, WIDTH), BF16),
            pltpu.VMEM((NC, 2, HF, WIDTH), BF16),
            pltpu.VMEM((NC, 2, CR, WIDTH), BF16),
            pltpu.VMEM((NC, 2, CR, WIDTH), BF16),
            sem((4,)),
            *[sem((5, NC))] * 4,
            *[sem((NC,))] * 2,
            *[sem((NC, 2))] * 4,
        ],
        compiler_params=pltpu.CompilerParams(
            collective_id=1, has_side_effects=True, vmem_limit_bytes=VMEM_LIMIT
        ),
        name="project",
    )(partial, lse, weight)


def shards(queries, keys, values, gates, out_weight):
    ctx = lax.axis_index("ctx")
    padded = jnp.zeros((8, 128), jnp.int32).at[0, : HQ * TOPK].set(gates.reshape(-1))
    qa, ka, va, ga, oc, lc = gather(queries, keys, values, padded)
    flat = ga[:, 0, : HQ * TOPK].reshape(-1)
    place = jnp.stack([ctx // NZ, ctx % NZ]).astype(jnp.int32)
    partial, lse = attend(flat, place, qa, ka, va, oc, lc)
    return project(partial, lse, out_weight)


def solution(mesh):
    return jax.shard_map(
        shards,
        mesh=mesh,
        in_specs=(
            P("ctx", "head"),
            P("ctx", "head"),
            P("ctx", "head"),
            P("ctx", "head", None),
            P("head", None),
        ),
        out_specs=P("ctx", "head"),
        check_vma=False,
    )
```

```python
import functools

import jax
import jax.numpy as jnp
from jax import lax
from jax.experimental import pallas as pl
from jax.experimental.pallas import tpu as pltpu
from jax.sharding import PartitionSpec as P

MESH = pl.DeviceIdType.MESH
F32 = jnp.float32
BF16 = jnp.bfloat16
TOK = 1024
HS = 128
HQ = 4
TOPK = 3
NY = 4
NZ = 8
NX = 4
SCALE2 = HS**-0.5 * 1.4426950408889634
LOW = -1e30
VMEM_LIMIT = 56 * 1024 * 1024
QCH = 4


RT = 256
NT = TOK // RT
SAFE = 2.0**100
WIDTH = HQ * HS
HALF = WIDTH // 2


def at(i):
    return pl.ds(i * RT, RT)


def wide(m, n):
    return jnp.concatenate([m] * (n // HS), axis=1)


def raw_scores(q, k):
    return lax.dot_general(q, k, (((1,), (1,)), ((), ())), preferred_element_type=F32)


def row_max(s):
    return jnp.broadcast_to(jnp.max(s, axis=1, keepdims=True) * SCALE2, (s.shape[0], HS))


def weights(s, m):
    return jnp.exp2(s * SCALE2 - wide(m, s.shape[1])).astype(BF16)


def as_row(m):
    eye = lax.broadcasted_iota(jnp.int32, (HS, HS), 0) == lax.broadcasted_iota(jnp.int32, (HS, HS), 1)
    pieces = [
        jnp.sum(jnp.where(eye, m[r : r + HS], 0.0), axis=0, keepdims=True) for r in range(0, m.shape[0], HS)
    ]
    return jnp.concatenate(pieces, axis=1)


def dev(ctx, head):
    return (ctx, head)


def gather_kernel(
    q_ref, k_ref, v_ref, g_ref, qa, ka, va, ga, oc, lc, vx, ov, lv, qt, kv_s, kv_r, q_s, q_r, g_s, g_r, loc, res
):
    ctx = lax.axis_index("ctx")
    head = lax.axis_index("head")
    y = ctx // NZ
    z = ctx % NZ
    up = y * NZ + (z + 1) % NZ
    down = y * NZ + (z + NZ - 1) % NZ
    column = [((y + d) % NY) * NZ + z for d in (1, 2, 3)]

    barrier = pltpu.get_barrier_semaphore()
    for other in [up, down] + column:
        pl.semaphore_signal(barrier, inc=1, device_id=dev(other, head), device_id_type=MESH)
    pl.semaphore_wait(barrier, 5)

    def remote(src, dst, s, r, to):
        return pltpu.make_async_remote_copy(
            src_ref=src, dst_ref=dst, send_sem=s, recv_sem=r, device_id=dev(to, head), device_id_type=MESH
        )

    def ring_copy(direction, step, part):
        block = (z + NZ - step) % NZ if direction == 0 else (z + step) % NZ
        own, out = (k_ref, ka) if part == 0 else (v_ref, va)
        src = own if step == 0 else out.at[block]
        return remote(
            src, out.at[block], kv_s.at[direction, step, part], kv_r.at[direction, step, part], up if direction == 0 else down
        )

    def parts(direction, step):
        return (0, 1) if step < 3 else (direction,)

    own_copies = [
        pltpu.make_async_copy(k_ref, ka.at[z], loc.at[0]),
        pltpu.make_async_copy(v_ref, va.at[z], loc.at[1]),
        pltpu.make_async_copy(q_ref, qa.at[0], loc.at[2]),
        pltpu.make_async_copy(g_ref, ga.at[0], loc.at[3]),
    ]
    rows = TOK // QCH
    above, below = column[0], column[2]
    second = pl.ds(HALF, HALF)
    first = pl.ds(0, HALF)

    def q_copy(kind, c):
        at_c = pl.ds(c * rows, rows)
        src, dst, to = (
            (q_ref.at[at_c], qa.at[1, at_c], below),
            (qa.at[1, at_c, first], qa.at[2, at_c, first], below),
            (q_ref.at[at_c], qa.at[3, at_c], above),
            (q_ref.at[at_c, second], qt.at[at_c], above),
            (qt.at[at_c], qa.at[2, at_c, second], above),
            (qa.at[3, at_c, second], qa.at[2, at_c, second], above),
        )[kind]
        return remote(src, dst, q_s.at[kind, c], q_r.at[kind, c], to)

    def q_start(r):
        @pl.when(y == 3)
        def _():
            q_copy(2, r).start()

        @pl.when(y >= 1)
        def _():
            q_copy(0, r).start()

        @pl.when(y == 2)
        def _():
            q_copy(3, r).start()

    def q_pass(r):
        @pl.when((y == 1) | (y == 2))
        def _():
            q_copy(0, r).wait_recv()
            q_copy(1, r).start()

        @pl.when(y == 3)
        def _():
            q_copy(3, r).wait_recv()
            q_copy(4, r).start()

        @pl.when(y == 0)
        def _():
            q_copy(2, r).wait_recv()
            q_copy(5, r).start()

    def q_end(r):
        @pl.when(y == 0)
        def _():
            q_copy(0, r).wait_recv()
            q_copy(4, r).wait_recv()
            q_copy(5, r).wait_send()

        @pl.when(y == 1)
        def _():
            q_copy(5, r).wait_recv()

        @pl.when(y <= 1)
        def _():
            q_copy(1, r).wait_recv()

        @pl.when(y >= 1)
        def _():
            q_copy(0, r).wait_send()

        @pl.when((y == 1) | (y == 2))
        def _():
            q_copy(1, r).wait_send()

        @pl.when(y == 2)
        def _():
            q_copy(3, r).wait_send()

        @pl.when(y == 3)
        def _():
            q_copy(2, r).wait_send()
            q_copy(4, r).wait_send()

    for part in (0, 1):
        for direction in (0, 1):
            ring_copy(direction, 0, part).start()

    for c in range(QCH):
        q_start(c)

    g_copies = [remote(g_ref, ga.at[NY - d], g_s.at[d - 1], g_r.at[d - 1], column[d - 1]) for d in (1, 2, 3)]
    for c in g_copies:
        c.start()
    for c in own_copies:
        c.start()

    vx[:, :HS] = v_ref[...]
    vx[:, HS:] = jnp.ones((TOK, HS), BF16)

    def result_copies(h):
        return [
            pltpu.make_async_copy(ov.at[:, pl.ds(h * HS, HS)], oc.at[:, pl.ds(h * HS, HS)], res.at[0, h]),
            pltpu.make_async_copy(lv.at[h], lc.at[h], res.at[1, h]),
        ]

    def causal(h):
        lanes = pl.ds(h * HS, HS)
        for i in range(NT):
            n = (i + 1) * RT
            s = raw_scores(q_ref[at(i), lanes], k_ref[0:n, :])
            r = lax.broadcasted_iota(jnp.int32, (RT, n), 0) + (n - RT)
            c = lax.broadcasted_iota(jnp.int32, (RT, n), 1)
            s = jnp.where(r >= c, s, LOW)
            m = row_max(s)
            mixed = jnp.dot(weights(s, m), vx[0:n, :], preferred_element_type=F32)
            total = mixed[:, HS:]
            ov[at(i), lanes] = (mixed[:, :HS] * (1.0 / total)).astype(BF16)
            lv[h, at(i), :] = m + jnp.log2(total)
        for c in result_copies(h):
            c.start()

    for step in range(4):
        for part in (0, 1):
            if 2 * step + part < HQ:
                causal(2 * step + part)
            for direction in (0, 1):
                if part in parts(direction, step):
                    ring_copy(direction, step, part).wait_recv()
                    if step < 3 and part in parts(direction, step + 1):
                        ring_copy(direction, step + 1, part).start()
        q_pass(step)

    for c in range(QCH):
        q_end(c)

    for step in range(4):
        for direction in (0, 1):
            for part in parts(direction, step):
                ring_copy(direction, step, part).wait_send()
    for c in g_copies:
        c.wait()
    for c in own_copies:
        c.wait()
    for h in range(HQ):
        for c in result_copies(h):
            c.wait()


def gather(q, k, v, g):
    hbm = pl.BlockSpec(memory_space=pl.ANY)
    return pl.pallas_call(
        gather_kernel,
        out_shape=(
            jax.ShapeDtypeStruct((NY, TOK, HQ * HS), BF16),
            jax.ShapeDtypeStruct((NZ, TOK, HS), BF16),
            jax.ShapeDtypeStruct((NZ, TOK, HS), BF16),
            jax.ShapeDtypeStruct((NY, HQ, TOPK), jnp.int32),
            jax.ShapeDtypeStruct((TOK, WIDTH), BF16),
            jax.ShapeDtypeStruct((HQ, TOK, HS), F32),
        ),
        in_specs=[pl.BlockSpec(memory_space=pltpu.VMEM)] * 4,
        out_specs=(hbm,) * 6,
        scratch_shapes=[
            pltpu.VMEM((TOK, 2 * HS), BF16),
            pltpu.VMEM((TOK, WIDTH), BF16),
            pltpu.VMEM((HQ, TOK, HS), F32),
            pltpu.VMEM((TOK, HALF), BF16),
            pltpu.SemaphoreType.DMA((2, 4, 2)),
            pltpu.SemaphoreType.DMA((2, 4, 2)),
            pltpu.SemaphoreType.DMA((6, QCH)),
            pltpu.SemaphoreType.DMA((6, QCH)),
            pltpu.SemaphoreType.DMA((3,)),
            pltpu.SemaphoreType.DMA((3,)),
            pltpu.SemaphoreType.DMA((4,)),
            pltpu.SemaphoreType.DMA((2, HQ)),
        ],
        compiler_params=pltpu.CompilerParams(
            collective_id=0, has_side_effects=True, vmem_limit_bytes=VMEM_LIMIT
        ),
        name="gather",
    )(q, k, v, g)


def attend_kernel(
    gates, q_hbm, k_hbm, v_hbm, oc_hbm, lc_hbm, out_hbm, lse_ref,
    q_ref, k_ref, vx, oc_ref, lc_ref, out_ref, peak, acc, largest, todo, sems, out_sems,
):
    ctx = lax.axis_index("ctx")
    y = ctx // NZ
    z = ctx % NZ

    keys_copy = pltpu.make_async_copy(k_hbm, k_ref, sems.at[0])
    values_copy = pltpu.make_async_copy(v_hbm, vx.at[:, :, pl.ds(0, HS)], sems.at[1])
    causal_copies = [
        pltpu.make_async_copy(oc_hbm, oc_ref, sems.at[2]),
        pltpu.make_async_copy(lc_hbm, lc_ref, sems.at[3]),
    ]

    def query_copy(slot):
        return pltpu.make_async_copy(q_hbm.at[slot], q_ref.at[slot], sems.at[4 + slot])

    def out_copy(slot):
        return pltpu.make_async_copy(out_ref.at[slot], out_hbm.at[slot], out_sems.at[slot])

    query_copy(1).start()
    keys_copy.start()
    values_copy.start()
    for slot in (2, 3, 0):
        query_copy(slot).start()
    for c in causal_copies:
        c.start()

    lse_ref[...] = jnp.full(lse_ref.shape, LOW, F32)
    largest[...] = jnp.zeros_like(largest)

    def fill(block, carry):
        vx[block, :, HS:] = jnp.ones((TOK, HS), BF16)
        return carry

    lax.fori_loop(0, NZ, fill, 0)
    keys_copy.wait()
    values_copy.wait()

    def one(index, general):
        slot = (index // HQ + 1) % NY
        head = index % HQ
        mine = (y + slot) * NZ + z
        lanes = pl.ds(pl.multiple_of(head * HS, HS), HS)

        if not general:

            @pl.when(head == 0)
            def _():
                query_copy(slot).wait()

            @pl.when((slot == 0) & (head == 0))
            def _():
                for c in causal_copies:
                    c.wait()

        def scores(i, block):
            return raw_scores(q_ref[slot, at(i), lanes], k_ref[block])

        def mix(s, m, block):
            return jnp.dot(weights(s, m), vx[block], preferred_element_type=F32)

        count = jnp.int32(0)
        for j in range(TOPK):
            g = gates[slot, head, j]
            good = (g >= y * NZ) & (g < (y + 1) * NZ) & (g < mine) & (y + slot < NY)

            @pl.when(good)
            def _(g=g, count=count):
                todo[count] = g - y * NZ

            count = count + good.astype(jnp.int32)

        def steady(e, carry):
            block = todo[e]
            for i in range(NT):
                acc[at(i), :] += mix(scores(i, block), peak[at(i), :], block)
            return carry

        def running(e, carry):
            block = todo[e]
            for i in range(NT):
                s = scores(i, block)
                old = peak[at(i), :]
                new = jnp.maximum(old, row_max(s))
                peak[at(i), :] = new
                acc[at(i), :] = acc[at(i), :] * wide(jnp.exp2(old - new), 2 * HS) + mix(s, new, block)
            return carry

        @pl.when(count > 0)
        def _():
            @pl.when(slot == 0)
            def _():
                peak[...] = lc_ref[head]
                acc[:, :HS] = oc_ref[:, lanes].astype(F32)
                acc[:, HS:] = jnp.ones((TOK, HS), F32)

            @pl.when(slot > 0)
            def _():
                if general:
                    peak[...] = jnp.full(peak.shape, LOW, F32)
                    acc[...] = jnp.zeros_like(acc)
                else:
                    block = todo[0]
                    for i in range(NT):
                        s = scores(i, block)
                        m = row_max(s[:, :RT])
                        peak[at(i), :] = m
                        acc[at(i), :] = mix(s, m, block)

            if general:
                lax.fori_loop(0, count, running, 0)
            else:
                lax.fori_loop(jnp.where(slot == 0, 0, 1), count, steady, 0)

            for i in range(NT):
                total = acc[at(i), HS:]
                largest[...] = jnp.maximum(largest[...], total)
                out_ref[slot, at(i), lanes] = (acc[at(i), :HS] * (1.0 / total)).astype(BF16)
                lse_ref[slot, pl.ds(head, 1), at(i)] = as_row(peak[at(i), :] + jnp.log2(total))

        @pl.when((count == 0) & (slot == 0))
        def _():
            out_ref[slot, :, lanes] = oc_ref[:, lanes]
            for i in range(NT):
                lse_ref[slot, pl.ds(head, 1), at(i)] = as_row(lc_ref[head, at(i), :])

        @pl.when((count == 0) & (slot > 0))
        def _():
            out_ref[slot, :, lanes] = jnp.zeros((TOK, HS), BF16)

        @pl.when(head == HQ - 1)
        def _():
            out_copy(slot).start()

    def run(general):
        def body(index, carry):
            one(index, general)
            return carry

        lax.fori_loop(0, NY * HQ, body, 0)
        for slot in range(NY):
            out_copy(slot).wait()

    run(False)

    @pl.when(jnp.logical_not(jnp.max(largest[...]) < SAFE))
    def _():
        run(True)


def attend(ga, qa, ka, va, oc, lc):
    hbm = pl.BlockSpec(memory_space=pl.ANY)
    return pl.pallas_call(
        attend_kernel,
        out_shape=(
            jax.ShapeDtypeStruct((NY, TOK, WIDTH), BF16),
            jax.ShapeDtypeStruct((NY, 8, TOK), F32),
        ),
        in_specs=[pl.BlockSpec(memory_space=pltpu.SMEM)] + [hbm] * 5,
        out_specs=(hbm, pl.BlockSpec(memory_space=pltpu.VMEM)),
        scratch_shapes=[
            pltpu.VMEM((NY, TOK, WIDTH), BF16),
            pltpu.VMEM((NZ, TOK, HS), BF16),
            pltpu.VMEM((NZ, TOK, 2 * HS), BF16),
            pltpu.VMEM((TOK, WIDTH), BF16),
            pltpu.VMEM((HQ, TOK, HS), F32),
            pltpu.VMEM((NY, TOK, WIDTH), BF16),
            pltpu.VMEM((TOK, HS), F32),
            pltpu.VMEM((TOK, 2 * HS), F32),
            pltpu.VMEM((RT, HS), F32),
            pltpu.SMEM((TOPK + 1,), jnp.int32),
            pltpu.SemaphoreType.DMA((4 + NY,)),
            pltpu.SemaphoreType.DMA((NY,)),
        ],
        compiler_params=pltpu.CompilerParams(vmem_limit_bytes=VMEM_LIMIT),
        name="attend",
    )(ga, qa, ka, va, oc, lc)


NC = 8
CR = TOK // NC
HF = CR // 2
LOOK = 3
LEFT_HALF = slice(0, HALF)
RIGHT_HALF = slice(HALF, WIDTH)


def join(sources, heads):
    top = functools.reduce(jnp.maximum, [l for l, _ in sources])
    ws = [jnp.exp2(l - top) for l, _ in sources]
    total = functools.reduce(jnp.add, ws)
    inv = 1.0 / total
    mixed = 0.0
    for w, (_, p) in zip(ws, sources):
        t = (w * inv).T
        wide_w = jnp.concatenate([jnp.broadcast_to(t[:, h : h + 1], (t.shape[0], HS)) for h in heads], axis=1)
        mixed = mixed + wide_w * p.astype(F32)
    return mixed.astype(BF16), top + jnp.log2(total)


def project_kernel(
    p_ref, l_ref, w_hbm, out_ref,
    w_ref, p0, p1, p3, r1, r2, r3, r4, r5, m1, m3, l1, l2, l3, l4, l5, lm1, lm3, att,
    sib_out, sib_in, own, a_out, a_in, b_out, b_in, out_rows,
    os, loc, ps, pr, ls, lr, ss, sr, as_, ar, bs, br,
):
    ctx = lax.axis_index("ctx")
    head = lax.axis_index("head")
    y = ctx // NZ
    z = ctx % NZ
    x = head // 2
    core = head % 2
    sibling = x * 2 + (1 - core)
    right = ((x + 1) % NX) * 2 + core
    left = ((x + NX - 1) % NX) * 2 + core
    beside = [right, left]
    above = ((y + 1) % NY) * NZ + z
    below = ((y + NY - 1) % NY) * NZ + z

    local = [
        pltpu.make_async_copy(p_ref.at[0], p0, loc.at[0]),
        pltpu.make_async_copy(p_ref.at[1], p1, loc.at[1]),
        pltpu.make_async_copy(p_ref.at[3], p3, loc.at[2]),
        pltpu.make_async_copy(w_hbm, w_ref, loc.at[3]),
    ]
    for c in local:
        c.start()

    barrier = pltpu.get_barrier_semaphore()
    for other in [(ctx, sibling), (ctx, right), (ctx, left), (above, head), (below, head)]:
        pl.semaphore_signal(barrier, inc=1, device_id=other, device_id_type=MESH)
    pl.semaphore_wait(barrier, 5)

    def remote(src, dst, s, r, to):
        return pltpu.make_async_remote_copy(
            src_ref=src, dst_ref=dst, send_sem=s, recv_sem=r, device_id=to, device_id_type=MESH
        )

    def rows_of(r):
        return pl.ds(pl.multiple_of(r * CR, CR), CR)

    def stream(kind, r, merged=False):
        at = rows_of(r)
        first, second = pl.ds(0, HALF), pl.ds(HALF, HALF)
        own_lse = l_ref.at[min(kind, 2) + 1 if kind != 2 else 2, :, at]
        if kind == 0:
            src, lsrc = (m1.at[at], lm1.at[r]) if merged else (p_ref.at[1, at], own_lse)
            dst, ldst = r1.at[at], l1.at[r]
        elif kind == 1:
            src, lsrc, dst, ldst = p_ref.at[2, at, first], own_lse, r2.at[at], l2.at[r]
        elif kind == 2:
            src, lsrc, dst, ldst = p_ref.at[2, at, second], own_lse, r4.at[at], l4.at[r]
        elif kind == 3:
            src, lsrc, dst, ldst = m3.at[at], lm3.at[r], r3.at[at], l3.at[r]
        else:
            src, lsrc, dst, ldst = r4.at[at], l4.at[r], r5.at[at], l5.at[r]
        to = (above if kind < 2 else below, head)
        return [
            remote(src, dst, ps.at[kind, r], pr.at[kind, r], to),
            remote(lsrc, ldst, ls.at[kind, r], lr.at[kind, r], to),
        ]

    def begin(copies):
        for c in copies:
            c.start()

    def arrived(copies):
        for c in copies:
            c.wait_recv()

    def l_own(slot, r):
        return l_ref[slot, :, rows_of(r)]

    def pick(low, high):
        rows = lax.broadcasted_iota(jnp.int32, low.shape, 0)
        return jnp.where(rows < HQ // 2, low, high)

    def send_plain(r):
        @pl.when(y < 2)
        def _():
            begin(stream(2, r))
            begin(stream(1, r))

        @pl.when(y == 0)
        def _():
            begin(stream(0, r))

    def relay(r):
        at = rows_of(r)

        @pl.when((y == 1) | (y == 2))
        def _():
            arrived(stream(1, r))
            mixed, lse = join([(l_own(1, r), p1[at, LEFT_HALF]), (l2[r], r2[at, :])], (0, 1))
            m1[at, LEFT_HALF] = mixed
            m1[at, RIGHT_HALF] = p1[at, RIGHT_HALF]
            lm1[r] = pick(lse, l_own(1, r))
            begin(stream(0, r, True))

        @pl.when(y == 0)
        def _():
            arrived(stream(2, r))
            mixed, lse = join([(l_own(3, r), p3[at, RIGHT_HALF]), (l4[r], r4[at, :])], (2, 3))
            m3[at, RIGHT_HALF] = mixed
            m3[at, LEFT_HALF] = p3[at, LEFT_HALF]
            lm3[r] = pick(l_own(3, r), lse)
            begin(stream(3, r))

        @pl.when(y == 3)
        def _():
            arrived(stream(2, r))
            begin(stream(4, r))

    def home(r):
        at = rows_of(r)

        @pl.when(y == 0)
        def _():
            att[...] = p0[at, :]

        @pl.when(y == 1)
        def _():
            arrived(stream(0, r))
            att[...] = join([(l_own(0, r), p0[at, :]), (l1[r], r1[at, :])], range(HQ))[0]

        @pl.when(y == 2)
        def _():
            arrived(stream(0, r) + stream(4, r))
            own_lse = l_own(0, r)
            att[:, LEFT_HALF] = join([(own_lse, p0[at, LEFT_HALF]), (l1[r], r1[at, LEFT_HALF])], (0, 1))[0]
            att[:, RIGHT_HALF] = join(
                [(own_lse, p0[at, RIGHT_HALF]), (l1[r], r1[at, RIGHT_HALF]), (l5[r], r5[at, :])], (2, 3)
            )[0]

        @pl.when(y == 3)
        def _():
            arrived(stream(0, r) + stream(3, r))
            att[...] = join([(l_own(0, r), p0[at, :]), (l1[r], r1[at, :]), (l3[r], r3[at, :])], range(HQ))[0]

    def sib_copy(r):
        return remote(sib_out.at[r], sib_in.at[r], ss.at[r], sr.at[r], (ctx, sibling))

    def a_copy(r, side):
        return remote(a_out.at[r, side], a_in.at[r, side], as_.at[r, side], ar.at[r, side], (ctx, beside[side]))

    def b_copy(r, side):
        return remote(b_out.at[r, side], b_in.at[r, side], bs.at[r, side], br.at[r, side], (ctx, beside[side]))

    def columns(k, c):
        return pl.ds(pl.multiple_of((((x + k) % NX) * 2 + c) * WIDTH, WIDTH), WIDTH)

    def stage0(r):
        home(r)
        rows = att[...]
        for k in range(NX):
            t = jnp.dot(rows, w_ref[:, columns(k, 1 - core)], preferred_element_type=F32)
            sib_out[r, k] = t.astype(BF16)
        sib_copy(r).start()

    def stage0_own(r):
        rows = att[...]
        for k in range(NX):
            own[r, k] = jnp.dot(rows, w_ref[:, columns(k, core)], preferred_element_type=F32).astype(BF16)

    def pair(r, k, at):
        return own[r, k, at, :].astype(F32) + sib_in[r, k, at, :].astype(F32)

    def stage1(r):
        sib_copy(r).wait_recv()
        for side in (0, 1):
            a_out[r, side] = pair(r, 2, pl.ds(side * HF, HF)).astype(BF16)
            a_copy(r, side).start()

    def stage2(r):
        for side in (0, 1):
            k = 1 if side == 0 else 3
            a_copy(r, side).wait_recv()
            with_a = pl.ds(side * HF, HF)
            without = pl.ds((1 - side) * HF, HF)
            b_out[r, side, with_a, :] = (pair(r, k, with_a) + a_in[r, side].astype(F32)).astype(BF16)
            b_out[r, side, without, :] = pair(r, k, without).astype(BF16)
            b_copy(r, side).start()

    def out_copy(r):
        return pltpu.make_async_copy(out_rows.at[r], out_ref.at[rows_of(r)], os.at[r])

    def stage3(r):
        b_copy(r, 0).wait_recv()
        b_copy(r, 1).wait_recv()
        total = pair(r, 0, pl.ds(0, CR)) + b_in[r, 0].astype(F32) + b_in[r, 1].astype(F32)
        out_rows[r] = total.astype(BF16)
        out_copy(r).start()

    def when(cond, f, r):
        @pl.when(cond)
        def _():
            f(r)

    for r in range(LOOK):
        send_plain(r)
    local[1].wait()
    local[2].wait()
    relay(0)
    local[0].wait()
    local[3].wait()

    def step(t, carry):
        when(t + LOOK < NC, send_plain, t + LOOK)
        when((t >= 1) & (t < NC + 1), stage1, t - 1)
        when((t >= 2) & (t < NC + 2), stage2, t - 2)
        when(t + 1 < NC, relay, t + 1)
        when(t < NC, stage0, t)
        when(t < NC, stage0_own, t)
        when(t >= 3, stage3, t - 3)
        return carry

    lax.fori_loop(0, NC + 3, step, 0)

    def sent(copies):
        for c in copies:
            c.wait_send()

    def finish(r, carry):
        @pl.when(y < 3)
        def _():
            sent(stream(0, r))

        @pl.when(y < 2)
        def _():
            sent(stream(1, r) + stream(2, r))

        @pl.when(y == 0)
        def _():
            sent(stream(3, r))

        @pl.when(y == 3)
        def _():
            sent(stream(4, r))

        out_copy(r).wait()
        sib_copy(r).wait_send()
        for side in (0, 1):
            a_copy(r, side).wait_send()
            b_copy(r, side).wait_send()
        return carry

    lax.fori_loop(0, NC, finish, 0)


def project(partial, lse, weight):
    vmem = pl.BlockSpec(memory_space=pltpu.VMEM)
    hbm = pl.BlockSpec(memory_space=pl.ANY)
    sem = pltpu.SemaphoreType.DMA
    full = pltpu.VMEM((TOK, WIDTH), BF16)
    half = pltpu.VMEM((TOK, HALF), BF16)
    return pl.pallas_call(
        project_kernel,
        out_shape=jax.ShapeDtypeStruct((TOK, WIDTH), BF16),
        in_specs=[hbm, vmem, hbm],
        out_specs=hbm,
        scratch_shapes=[
            pltpu.VMEM(weight.shape, BF16),
            full, full, full,
            full, half, full, half, half,
            full, full,
            *[pltpu.VMEM((NC, 8, CR), F32)] * 7,
            pltpu.VMEM((CR, WIDTH), BF16),
            pltpu.VMEM((NC, NX, CR, WIDTH), BF16),
            pltpu.VMEM((NC, NX, CR, WIDTH), BF16),
            pltpu.VMEM((NC, NX, CR, WIDTH), BF16),
            pltpu.VMEM((NC, 2, HF, WIDTH), BF16),
            pltpu.VMEM((NC, 2, HF, WIDTH), BF16),
            pltpu.VMEM((NC, 2, CR, WIDTH), BF16),
            pltpu.VMEM((NC, 2, CR, WIDTH), BF16),
            pltpu.VMEM((NC, CR, WIDTH), BF16),
            sem((NC,)),
            sem((4,)),
            *[sem((5, NC))] * 4,
            *[sem((NC,))] * 2,
            *[sem((NC, 2))] * 4,
        ],
        compiler_params=pltpu.CompilerParams(
            collective_id=1, has_side_effects=True, vmem_limit_bytes=VMEM_LIMIT
        ),
        name="project",
    )(partial, lse, weight)


def shards(queries, keys, values, gates, out_weight):
    qa, ka, va, ga, oc, lc = gather(queries, keys, values, gates[0])
    partial, lse = attend(ga, qa, ka, va, oc, lc)
    return project(partial, lse, out_weight)


def solution(mesh):
    return jax.shard_map(
        shards,
        mesh=mesh,
        in_specs=(
            P("ctx", "head"),
            P("ctx", "head"),
            P("ctx", "head"),
            P("ctx", "head", None),
            P("head", None),
        ),
        out_specs=P("ctx", "head"),
        check_vma=False,
    )
```

```python
import functools

import jax
import jax.numpy as jnp
from jax import lax
from jax.experimental import pallas as pl
from jax.experimental.pallas import tpu as pltpu
from jax.sharding import PartitionSpec as P

MESH = pl.DeviceIdType.MESH
F32 = jnp.float32
BF16 = jnp.bfloat16
TOK = 1024
HS = 128
HQ = 4
TOPK = 3
NY = 4
NZ = 8
NX = 4
SCALE2 = HS**-0.5 * 1.4426950408889634
LOW = -1e30
VMEM_LIMIT = 56 * 1024 * 1024
QCH = 4


RT = 256
NT = TOK // RT
SAFE = 2.0**100
WIDTH = HQ * HS
HALF = WIDTH // 2


def at(i):
    return pl.ds(i * RT, RT)


def wide(m, n):
    return jnp.concatenate([m] * (n // HS), axis=1)


def raw_scores(q, k):
    return lax.dot_general(q, k, (((1,), (1,)), ((), ())), preferred_element_type=F32)


def row_max(s):
    return jnp.broadcast_to(jnp.max(s, axis=1, keepdims=True) * SCALE2, (s.shape[0], HS))


def weights(s, m):
    return jnp.exp2(s * SCALE2 - wide(m, s.shape[1])).astype(BF16)


def as_row(m):
    eye = lax.broadcasted_iota(jnp.int32, (HS, HS), 0) == lax.broadcasted_iota(jnp.int32, (HS, HS), 1)
    pieces = [
        jnp.sum(jnp.where(eye, m[r : r + HS], 0.0), axis=0, keepdims=True) for r in range(0, m.shape[0], HS)
    ]
    return jnp.concatenate(pieces, axis=1)


def dev(ctx, head):
    return (ctx, head)


def gather_kernel(
    q_ref, k_ref, v_ref, g_ref, qa, ka, va, ga, oc, lc, vx, ov, lv, qt, kv_s, kv_r, q_s, q_r, g_s, g_r, loc, res
):
    ctx = lax.axis_index("ctx")
    head = lax.axis_index("head")
    y = ctx // NZ
    z = ctx % NZ
    up = y * NZ + (z + 1) % NZ
    down = y * NZ + (z + NZ - 1) % NZ
    column = [((y + d) % NY) * NZ + z for d in (1, 2, 3)]

    barrier = pltpu.get_barrier_semaphore()
    for other in [up, down] + column:
        pl.semaphore_signal(barrier, inc=1, device_id=dev(other, head), device_id_type=MESH)
    pl.semaphore_wait(barrier, 5)

    def remote(src, dst, s, r, to):
        return pltpu.make_async_remote_copy(
            src_ref=src, dst_ref=dst, send_sem=s, recv_sem=r, device_id=dev(to, head), device_id_type=MESH
        )

    def ring_copy(direction, step, part):
        block = (z + NZ - step) % NZ if direction == 0 else (z + step) % NZ
        own, out = (k_ref, ka) if part == 0 else (v_ref, va)
        src = own if step == 0 else out.at[block]
        return remote(
            src, out.at[block], kv_s.at[direction, step, part], kv_r.at[direction, step, part], up if direction == 0 else down
        )

    def parts(direction, step):
        return (0, 1) if step < 3 else (direction,)

    own_copies = [
        pltpu.make_async_copy(k_ref, ka.at[z], loc.at[0]),
        pltpu.make_async_copy(v_ref, va.at[z], loc.at[1]),
        pltpu.make_async_copy(q_ref, qa.at[0], loc.at[2]),
        pltpu.make_async_copy(g_ref, ga.at[0], loc.at[3]),
    ]
    rows = TOK // QCH
    above, below = column[0], column[2]
    second = pl.ds(HALF, HALF)
    first = pl.ds(0, HALF)

    def q_copy(kind, c):
        at_c = pl.ds(c * rows, rows)
        src, dst, to = (
            (q_ref.at[at_c], qa.at[1, at_c], below),
            (qa.at[1, at_c, first], qa.at[2, at_c, first], below),
            (q_ref.at[at_c], qa.at[3, at_c], above),
            (q_ref.at[at_c, second], qt.at[at_c], above),
            (qt.at[at_c], qa.at[2, at_c, second], above),
            (qa.at[3, at_c, second], qa.at[2, at_c, second], above),
        )[kind]
        return remote(src, dst, q_s.at[kind, c], q_r.at[kind, c], to)

    def q_start(r):
        @pl.when(y == 3)
        def _():
            q_copy(2, r).start()

        @pl.when(y >= 1)
        def _():
            q_copy(0, r).start()

        @pl.when(y == 2)
        def _():
            q_copy(3, r).start()

    def q_pass(r):
        @pl.when((y == 1) | (y == 2))
        def _():
            q_copy(0, r).wait_recv()
            q_copy(1, r).start()

        @pl.when(y == 3)
        def _():
            q_copy(3, r).wait_recv()
            q_copy(4, r).start()

        @pl.when(y == 0)
        def _():
            q_copy(2, r).wait_recv()
            q_copy(5, r).start()

    def q_end(r):
        @pl.when(y == 0)
        def _():
            q_copy(0, r).wait_recv()
            q_copy(4, r).wait_recv()
            q_copy(5, r).wait_send()

        @pl.when(y == 1)
        def _():
            q_copy(5, r).wait_recv()

        @pl.when(y <= 1)
        def _():
            q_copy(1, r).wait_recv()

        @pl.when(y >= 1)
        def _():
            q_copy(0, r).wait_send()

        @pl.when((y == 1) | (y == 2))
        def _():
            q_copy(1, r).wait_send()

        @pl.when(y == 2)
        def _():
            q_copy(3, r).wait_send()

        @pl.when(y == 3)
        def _():
            q_copy(2, r).wait_send()
            q_copy(4, r).wait_send()

    for part in (0, 1):
        for direction in (0, 1):
            ring_copy(direction, 0, part).start()

    for c in range(QCH):
        q_start(c)

    g_copies = [remote(g_ref, ga.at[NY - d], g_s.at[d - 1], g_r.at[d - 1], column[d - 1]) for d in (1, 2, 3)]
    for c in g_copies:
        c.start()
    for c in own_copies:
        c.start()

    vx[:, :HS] = v_ref[...]
    vx[:, HS:] = jnp.ones((TOK, HS), BF16)

    def result_copies(h):
        return [
            pltpu.make_async_copy(ov.at[:, pl.ds(h * HS, HS)], oc.at[:, pl.ds(h * HS, HS)], res.at[0, h]),
            pltpu.make_async_copy(lv.at[h], lc.at[h], res.at[1, h]),
        ]

    def causal(h):
        lanes = pl.ds(h * HS, HS)
        for i in range(NT):
            n = (i + 1) * RT
            s = raw_scores(q_ref[at(i), lanes], k_ref[0:n, :])
            r = lax.broadcasted_iota(jnp.int32, (RT, n), 0) + (n - RT)
            c = lax.broadcasted_iota(jnp.int32, (RT, n), 1)
            s = jnp.where(r >= c, s, LOW)
            m = row_max(s)
            mixed = jnp.dot(weights(s, m), vx[0:n, :], preferred_element_type=F32)
            total = mixed[:, HS:]
            ov[at(i), lanes] = (mixed[:, :HS] * (1.0 / total)).astype(BF16)
            lv[h, at(i), :] = m + jnp.log2(total)
        for c in result_copies(h):
            c.start()

    for step in range(4):
        for part in (0, 1):
            if 2 * step + part < HQ:
                causal(2 * step + part)
            for direction in (0, 1):
                if part in parts(direction, step):
                    ring_copy(direction, step, part).wait_recv()
                    if step < 3 and part in parts(direction, step + 1):
                        ring_copy(direction, step + 1, part).start()
        q_pass(step)

    for c in range(QCH):
        q_end(c)

    for step in range(4):
        for direction in (0, 1):
            for part in parts(direction, step):
                ring_copy(direction, step, part).wait_send()
    for c in g_copies:
        c.wait()
    for c in own_copies:
        c.wait()
    for h in range(HQ):
        for c in result_copies(h):
            c.wait()


def gather(q, k, v, g):
    hbm = pl.BlockSpec(memory_space=pl.ANY)
    return pl.pallas_call(
        gather_kernel,
        out_shape=(
            jax.ShapeDtypeStruct((NY, TOK, HQ * HS), BF16),
            jax.ShapeDtypeStruct((NZ, TOK, HS), BF16),
            jax.ShapeDtypeStruct((NZ, TOK, HS), BF16),
            jax.ShapeDtypeStruct((NY, HQ, TOPK), jnp.int32),
            jax.ShapeDtypeStruct((TOK, WIDTH), BF16),
            jax.ShapeDtypeStruct((HQ, TOK, HS), F32),
        ),
        in_specs=[pl.BlockSpec(memory_space=pltpu.VMEM)] * 4,
        out_specs=(hbm,) * 6,
        scratch_shapes=[
            pltpu.VMEM((TOK, 2 * HS), BF16),
            pltpu.VMEM((TOK, WIDTH), BF16),
            pltpu.VMEM((HQ, TOK, HS), F32),
            pltpu.VMEM((TOK, HALF), BF16),
            pltpu.SemaphoreType.DMA((2, 4, 2)),
            pltpu.SemaphoreType.DMA((2, 4, 2)),
            pltpu.SemaphoreType.DMA((6, QCH)),
            pltpu.SemaphoreType.DMA((6, QCH)),
            pltpu.SemaphoreType.DMA((3,)),
            pltpu.SemaphoreType.DMA((3,)),
            pltpu.SemaphoreType.DMA((4,)),
            pltpu.SemaphoreType.DMA((2, HQ)),
        ],
        compiler_params=pltpu.CompilerParams(
            collective_id=0, has_side_effects=True, vmem_limit_bytes=VMEM_LIMIT
        ),
        name="gather",
    )(q, k, v, g)


def attend_kernel(
    gates, q_hbm, k_hbm, v_hbm, oc_hbm, lc_hbm, out_hbm, lse_ref,
    q_ref, k_ref, vx, oc_ref, lc_ref, out_ref, peak, acc, largest, todo, sems, out_sems,
):
    ctx = lax.axis_index("ctx")
    y = ctx // NZ
    z = ctx % NZ

    keys_copy = pltpu.make_async_copy(k_hbm, k_ref, sems.at[0])
    values_copy = pltpu.make_async_copy(v_hbm, vx.at[:, :, pl.ds(0, HS)], sems.at[1])
    causal_copies = [
        pltpu.make_async_copy(oc_hbm, oc_ref, sems.at[2]),
        pltpu.make_async_copy(lc_hbm, lc_ref, sems.at[3]),
    ]

    def query_copy(slot):
        return pltpu.make_async_copy(q_hbm.at[slot], q_ref.at[slot], sems.at[4 + slot])

    def out_copy(slot):
        return pltpu.make_async_copy(out_ref.at[slot], out_hbm.at[slot], out_sems.at[slot])

    query_copy(1).start()
    keys_copy.start()
    values_copy.start()
    for slot in (2, 3, 0):
        query_copy(slot).start()
    for c in causal_copies:
        c.start()

    lse_ref[...] = jnp.full(lse_ref.shape, LOW, F32)
    largest[...] = jnp.zeros_like(largest)

    def fill(block, carry):
        vx[block, :, HS:] = jnp.ones((TOK, HS), BF16)
        return carry

    lax.fori_loop(0, NZ, fill, 0)
    keys_copy.wait()
    values_copy.wait()

    def one(index, general):
        slot = (index // HQ + 1) % NY
        head = index % HQ
        mine = (y + slot) * NZ + z
        lanes = pl.ds(pl.multiple_of(head * HS, HS), HS)

        if not general:

            @pl.when(head == 0)
            def _():
                query_copy(slot).wait()

            @pl.when((slot == 0) & (head == 0))
            def _():
                for c in causal_copies:
                    c.wait()

        def scores(i, block):
            return raw_scores(q_ref[slot, at(i), lanes], k_ref[block])

        def mix(s, m, block):
            return jnp.dot(weights(s, m), vx[block], preferred_element_type=F32)

        count = jnp.int32(0)
        for j in range(TOPK):
            g = gates[slot, head, j]
            good = (g >= y * NZ) & (g < (y + 1) * NZ) & (g < mine) & (y + slot < NY)
            todo[count] = g - y * NZ
            count = count + good.astype(jnp.int32)

        def steady(e, carry):
            block = todo[e]
            ahead = scores(0, block)
            for i in range(NT):
                s = ahead
                if i + 1 < NT:
                    ahead = scores(i + 1, block)
                acc[at(i), :] += mix(s, peak[at(i), :], block)
            return carry

        def running(e, carry):
            block = todo[e]
            for i in range(NT):
                s = scores(i, block)
                old = peak[at(i), :]
                new = jnp.maximum(old, row_max(s))
                peak[at(i), :] = new
                acc[at(i), :] = acc[at(i), :] * wide(jnp.exp2(old - new), 2 * HS) + mix(s, new, block)
            return carry

        @pl.when(count > 0)
        def _():
            @pl.when(slot == 0)
            def _():
                peak[...] = lc_ref[head]
                acc[:, :HS] = oc_ref[:, lanes].astype(F32)
                acc[:, HS:] = jnp.ones((TOK, HS), F32)

            @pl.when(slot > 0)
            def _():
                if general:
                    peak[...] = jnp.full(peak.shape, LOW, F32)
                    acc[...] = jnp.zeros_like(acc)
                else:
                    block = todo[0]
                    ahead = scores(0, block)
                    for i in range(NT):
                        s = ahead
                        if i + 1 < NT:
                            ahead = scores(i + 1, block)
                        m = row_max(s[:, :RT])
                        peak[at(i), :] = m
                        acc[at(i), :] = mix(s, m, block)

            if general:
                lax.fori_loop(0, count, running, 0)
            else:
                lax.fori_loop(jnp.where(slot == 0, 0, 1), count, steady, 0)

            for i in range(NT):
                total = acc[at(i), HS:]
                largest[...] = jnp.maximum(largest[...], total)
                out_ref[slot, at(i), lanes] = (acc[at(i), :HS] * (1.0 / total)).astype(BF16)
                lse_ref[slot, pl.ds(head, 1), at(i)] = as_row(peak[at(i), :] + jnp.log2(total))

        @pl.when((count == 0) & (slot == 0))
        def _():
            out_ref[slot, :, lanes] = oc_ref[:, lanes]
            for i in range(NT):
                lse_ref[slot, pl.ds(head, 1), at(i)] = as_row(lc_ref[head, at(i), :])

        @pl.when((count == 0) & (slot > 0))
        def _():
            out_ref[slot, :, lanes] = jnp.zeros((TOK, HS), BF16)

        @pl.when(head == HQ - 1)
        def _():
            out_copy(slot).start()

    def run(general):
        def body(index, carry):
            one(index, general)
            return carry

        lax.fori_loop(0, NY * HQ, body, 0)
        for slot in range(NY):
            out_copy(slot).wait()

    run(False)

    @pl.when(jnp.logical_not(jnp.max(largest[...]) < SAFE))
    def _():
        run(True)


def attend(ga, qa, ka, va, oc, lc):
    hbm = pl.BlockSpec(memory_space=pl.ANY)
    return pl.pallas_call(
        attend_kernel,
        out_shape=(
            jax.ShapeDtypeStruct((NY, TOK, WIDTH), BF16),
            jax.ShapeDtypeStruct((NY, 8, TOK), F32),
        ),
        in_specs=[pl.BlockSpec(memory_space=pltpu.SMEM)] + [hbm] * 5,
        out_specs=(hbm, pl.BlockSpec(memory_space=pltpu.VMEM)),
        scratch_shapes=[
            pltpu.VMEM((NY, TOK, WIDTH), BF16),
            pltpu.VMEM((NZ, TOK, HS), BF16),
            pltpu.VMEM((NZ, TOK, 2 * HS), BF16),
            pltpu.VMEM((TOK, WIDTH), BF16),
            pltpu.VMEM((HQ, TOK, HS), F32),
            pltpu.VMEM((NY, TOK, WIDTH), BF16),
            pltpu.VMEM((TOK, HS), F32),
            pltpu.VMEM((TOK, 2 * HS), F32),
            pltpu.VMEM((RT, HS), F32),
            pltpu.SMEM((TOPK + 1,), jnp.int32),
            pltpu.SemaphoreType.DMA((4 + NY,)),
            pltpu.SemaphoreType.DMA((NY,)),
        ],
        compiler_params=pltpu.CompilerParams(vmem_limit_bytes=VMEM_LIMIT),
        name="attend",
    )(ga, qa, ka, va, oc, lc)


NC = 8
CR = TOK // NC
HF = CR // 2
LOOK = 2
LEFT_HALF = slice(0, HALF)
RIGHT_HALF = slice(HALF, WIDTH)


def join(sources, heads):
    top = functools.reduce(jnp.maximum, [l for l, _ in sources])
    ws = [jnp.exp2(l - top) for l, _ in sources]
    total = functools.reduce(jnp.add, ws)
    inv = 1.0 / total
    mixed = 0.0
    for w, (_, p) in zip(ws, sources):
        t = (w * inv).T
        wide_w = jnp.concatenate([jnp.broadcast_to(t[:, h : h + 1], (t.shape[0], HS)) for h in heads], axis=1)
        mixed = mixed + wide_w * p.astype(F32)
    return mixed.astype(BF16), top + jnp.log2(total)


def project_kernel(
    p_ref, l_ref, w_hbm, out_ref,
    w_ref, p0, p1, p3, r1, r2, r3, r4, r5, m1, m3, l1, l2, l3, l4, l5, lm1, lm3, att,
    sib_out, sib_in, own, a_out, a_in, b_out, b_in, out_rows,
    os, loc, ps, pr, ls, lr, ss, sr, as_, ar, bs, br,
):
    ctx = lax.axis_index("ctx")
    head = lax.axis_index("head")
    y = ctx // NZ
    z = ctx % NZ
    x = head // 2
    core = head % 2
    sibling = x * 2 + (1 - core)
    right = ((x + 1) % NX) * 2 + core
    left = ((x + NX - 1) % NX) * 2 + core
    beside = [right, left]
    above = ((y + 1) % NY) * NZ + z
    below = ((y + NY - 1) % NY) * NZ + z

    local = [
        pltpu.make_async_copy(p_ref.at[0], p0, loc.at[0]),
        pltpu.make_async_copy(p_ref.at[1], p1, loc.at[1]),
        pltpu.make_async_copy(p_ref.at[3], p3, loc.at[2]),
        pltpu.make_async_copy(w_hbm, w_ref, loc.at[3]),
    ]
    for c in local:
        c.start()

    barrier = pltpu.get_barrier_semaphore()
    for other in [(ctx, sibling), (ctx, right), (ctx, left), (above, head), (below, head)]:
        pl.semaphore_signal(barrier, inc=1, device_id=other, device_id_type=MESH)
    pl.semaphore_wait(barrier, 5)

    def remote(src, dst, s, r, to):
        return pltpu.make_async_remote_copy(
            src_ref=src, dst_ref=dst, send_sem=s, recv_sem=r, device_id=to, device_id_type=MESH
        )

    def rows_of(r):
        return pl.ds(pl.multiple_of(r * CR, CR), CR)

    def stream(kind, r, merged=False):
        at = rows_of(r)
        first, second = pl.ds(0, HALF), pl.ds(HALF, HALF)
        own_lse = l_ref.at[min(kind, 2) + 1 if kind != 2 else 2, :, at]
        if kind == 0:
            src, lsrc = (m1.at[at], lm1.at[r]) if merged else (p_ref.at[1, at], own_lse)
            dst, ldst = r1.at[at], l1.at[r]
        elif kind == 1:
            src, lsrc, dst, ldst = p_ref.at[2, at, first], own_lse, r2.at[at], l2.at[r]
        elif kind == 2:
            src, lsrc, dst, ldst = p_ref.at[2, at, second], own_lse, r4.at[at], l4.at[r]
        elif kind == 3:
            src, lsrc, dst, ldst = m3.at[at], lm3.at[r], r3.at[at], l3.at[r]
        else:
            src, lsrc, dst, ldst = r4.at[at], l4.at[r], r5.at[at], l5.at[r]
        to = (above if kind < 2 else below, head)
        return [
            remote(src, dst, ps.at[kind, r], pr.at[kind, r], to),
            remote(lsrc, ldst, ls.at[kind, r], lr.at[kind, r], to),
        ]

    def begin(copies):
        for c in copies:
            c.start()

    def arrived(copies):
        for c in copies:
            c.wait_recv()

    def l_own(slot, r):
        return l_ref[slot, :, rows_of(r)]

    def pick(low, high):
        rows = lax.broadcasted_iota(jnp.int32, low.shape, 0)
        return jnp.where(rows < HQ // 2, low, high)

    def send_plain(r):
        @pl.when(y < 2)
        def _():
            begin(stream(2, r))
            begin(stream(1, r))

        @pl.when(y == 0)
        def _():
            begin(stream(0, r))

    def relay(r):
        at = rows_of(r)

        @pl.when((y == 1) | (y == 2))
        def _():
            arrived(stream(1, r))
            mixed, lse = join([(l_own(1, r), p1[at, LEFT_HALF]), (l2[r], r2[at, :])], (0, 1))
            m1[at, LEFT_HALF] = mixed
            m1[at, RIGHT_HALF] = p1[at, RIGHT_HALF]
            lm1[r] = pick(lse, l_own(1, r))
            begin(stream(0, r, True))

        @pl.when(y == 0)
        def _():
            arrived(stream(2, r))
            mixed, lse = join([(l_own(3, r), p3[at, RIGHT_HALF]), (l4[r], r4[at, :])], (2, 3))
            m3[at, RIGHT_HALF] = mixed
            m3[at, LEFT_HALF] = p3[at, LEFT_HALF]
            lm3[r] = pick(l_own(3, r), lse)
            begin(stream(3, r))

        @pl.when(y == 3)
        def _():
            arrived(stream(2, r))
            begin(stream(4, r))

    def home(r):
        at = rows_of(r)

        @pl.when(y == 0)
        def _():
            att[...] = p0[at, :]

        @pl.when(y == 1)
        def _():
            arrived(stream(0, r))
            att[...] = join([(l_own(0, r), p0[at, :]), (l1[r], r1[at, :])], range(HQ))[0]

        @pl.when(y == 2)
        def _():
            arrived(stream(0, r) + stream(4, r))
            own_lse = l_own(0, r)
            att[:, LEFT_HALF] = join([(own_lse, p0[at, LEFT_HALF]), (l1[r], r1[at, LEFT_HALF])], (0, 1))[0]
            att[:, RIGHT_HALF] = join(
                [(own_lse, p0[at, RIGHT_HALF]), (l1[r], r1[at, RIGHT_HALF]), (l5[r], r5[at, :])], (2, 3)
            )[0]

        @pl.when(y == 3)
        def _():
            arrived(stream(0, r) + stream(3, r))
            att[...] = join([(l_own(0, r), p0[at, :]), (l1[r], r1[at, :]), (l3[r], r3[at, :])], range(HQ))[0]

    def sib_copy(r):
        return remote(sib_out.at[r], sib_in.at[r], ss.at[r], sr.at[r], (ctx, sibling))

    def a_copy(r, side):
        return remote(a_out.at[r, side], a_in.at[r, side], as_.at[r, side], ar.at[r, side], (ctx, beside[side]))

    def b_copy(r, side):
        return remote(b_out.at[r, side], b_in.at[r, side], bs.at[r, side], br.at[r, side], (ctx, beside[side]))

    def columns(k, c):
        return pl.ds(pl.multiple_of((((x + k) % NX) * 2 + c) * WIDTH, WIDTH), WIDTH)

    def stage0(r):
        home(r)
        rows = att[...]
        for k in range(NX):
            t = jnp.dot(rows, w_ref[:, columns(k, 1 - core)], preferred_element_type=F32)
            sib_out[r, k] = t.astype(BF16)
        sib_copy(r).start()

    def stage0_own(r):
        rows = att[...]
        for k in range(NX):
            own[r, k] = jnp.dot(rows, w_ref[:, columns(k, core)], preferred_element_type=F32).astype(BF16)

    def pair(r, k, at):
        return own[r, k, at, :].astype(F32) + sib_in[r, k, at, :].astype(F32)

    def stage1(r):
        sib_copy(r).wait_recv()
        for side in (0, 1):
            a_out[r, side] = pair(r, 2, pl.ds(side * HF, HF)).astype(BF16)
            a_copy(r, side).start()

    def stage2(r):
        for side in (0, 1):
            k = 1 if side == 0 else 3
            a_copy(r, side).wait_recv()
            with_a = pl.ds(side * HF, HF)
            without = pl.ds((1 - side) * HF, HF)
            b_out[r, side, with_a, :] = (pair(r, k, with_a) + a_in[r, side].astype(F32)).astype(BF16)
            b_out[r, side, without, :] = pair(r, k, without).astype(BF16)
            b_copy(r, side).start()

    def out_copy(r):
        return pltpu.make_async_copy(out_rows.at[r], out_ref.at[rows_of(r)], os.at[r])

    def stage3(r):
        b_copy(r, 0).wait_recv()
        b_copy(r, 1).wait_recv()
        total = pair(r, 0, pl.ds(0, CR)) + b_in[r, 0].astype(F32) + b_in[r, 1].astype(F32)
        out_rows[r] = total.astype(BF16)
        out_copy(r).start()

    def when(cond, f, r):
        @pl.when(cond)
        def _():
            f(r)

    for r in range(LOOK):
        send_plain(r)
    local[1].wait()
    local[2].wait()
    relay(0)
    local[0].wait()
    local[3].wait()

    def step(t, carry):
        when(t + LOOK < NC, send_plain, t + LOOK)
        when((t >= 1) & (t < NC + 1), stage1, t - 1)
        when((t >= 2) & (t < NC + 2), stage2, t - 2)
        when(t + 1 < NC, relay, t + 1)
        when(t < NC, stage0, t)
        when(t < NC, stage0_own, t)
        when(t >= 3, stage3, t - 3)
        return carry

    lax.fori_loop(0, NC + 3, step, 0)

    def sent(copies):
        for c in copies:
            c.wait_send()

    def finish(r, carry):
        @pl.when(y < 3)
        def _():
            sent(stream(0, r))

        @pl.when(y < 2)
        def _():
            sent(stream(1, r) + stream(2, r))

        @pl.when(y == 0)
        def _():
            sent(stream(3, r))

        @pl.when(y == 3)
        def _():
            sent(stream(4, r))

        out_copy(r).wait()
        sib_copy(r).wait_send()
        for side in (0, 1):
            a_copy(r, side).wait_send()
            b_copy(r, side).wait_send()
        return carry

    lax.fori_loop(0, NC, finish, 0)


def project(partial, lse, weight):
    vmem = pl.BlockSpec(memory_space=pltpu.VMEM)
    hbm = pl.BlockSpec(memory_space=pl.ANY)
    sem = pltpu.SemaphoreType.DMA
    full = pltpu.VMEM((TOK, WIDTH), BF16)
    half = pltpu.VMEM((TOK, HALF), BF16)
    return pl.pallas_call(
        project_kernel,
        out_shape=jax.ShapeDtypeStruct((TOK, WIDTH), BF16),
        in_specs=[hbm, vmem, hbm],
        out_specs=hbm,
        scratch_shapes=[
            pltpu.VMEM(weight.shape, BF16),
            full, full, full,
            full, half, full, half, half,
            full, full,
            *[pltpu.VMEM((NC, 8, CR), F32)] * 7,
            pltpu.VMEM((CR, WIDTH), BF16),
            pltpu.VMEM((NC, NX, CR, WIDTH), BF16),
            pltpu.VMEM((NC, NX, CR, WIDTH), BF16),
            pltpu.VMEM((NC, NX, CR, WIDTH), BF16),
            pltpu.VMEM((NC, 2, HF, WIDTH), BF16),
            pltpu.VMEM((NC, 2, HF, WIDTH), BF16),
            pltpu.VMEM((NC, 2, CR, WIDTH), BF16),
            pltpu.VMEM((NC, 2, CR, WIDTH), BF16),
            pltpu.VMEM((NC, CR, WIDTH), BF16),
            sem((NC,)),
            sem((4,)),
            *[sem((5, NC))] * 4,
            *[sem((NC,))] * 2,
            *[sem((NC, 2))] * 4,
        ],
        compiler_params=pltpu.CompilerParams(
            collective_id=1, has_side_effects=True, vmem_limit_bytes=VMEM_LIMIT
        ),
        name="project",
    )(partial, lse, weight)


def shards(queries, keys, values, gates, out_weight):
    qa, ka, va, ga, oc, lc = gather(queries, keys, values, gates[0])
    partial, lse = attend(ga, qa, ka, va, oc, lc)
    return project(partial, lse, out_weight)


def solution(mesh):
    return jax.shard_map(
        shards,
        mesh=mesh,
        in_specs=(
            P("ctx", "head"),
            P("ctx", "head"),
            P("ctx", "head"),
            P("ctx", "head", None),
            P("head", None),
        ),
        out_specs=P("ctx", "head"),
        check_vma=False,
    )
```
